32 devices in a mesh: dp: 4 (over y, core), seq: 8 (over z, x).
Axes of the slice: x: 2, y: 2, z: 4, core: 2. Of those that a mesh axis runs over, the one named last changes fastest.
Arguments:
- tokens: bfloat16 [2048, 16, 768], P('seq', 'dp'), may hold values from -6 to 6
- cotangent: bfloat16 [2048, 16, 768], P('seq', 'dp'), may hold values from -6 to 6
- picked_ids: int32 [16, 256], P('dp'), may hold values from 0 to 2047, as said below
- lengths: int32 [16], P('dp'), may hold values from 1024 to 2048, as said below
- qkv_w: float32 [2, 3, 768, 768], P(None, None, ('dp', 'seq')), may hold values from -0.21875 to 0.21875
- out_w: float32 [2, 768, 768], P(None, ('dp', 'seq')), may hold values from -3.5 to 3.5
- up_w: float32 [2, 768, 3072], P(None, ('dp', 'seq')), may hold values from -0.21875 to 0.21875
- down_w: float32 [2, 3072, 768], P(None, ('dp', 'seq')), may hold values from -0.109375 to 0.109375
- vectors: float32 [5, 768], P(None, ('dp', 'seq')), may hold values from -1 to 3, as said below
- qkv_mom: float32 [2, 3, 768, 768], P(None, None, ('dp', 'seq')), may hold values from -0.00390625 to 0.00390625
- out_mom: float32 [2, 768, 768], P(None, ('dp', 'seq')), may hold values from -0.00390625 to 0.00390625
- up_mom: float32 [2, 768, 3072], P(None, ('dp', 'seq')), may hold values from -0.00390625 to 0.00390625
- down_mom: float32 [2, 3072, 768], P(None, ('dp', 'seq')), may hold values from -0.00390625 to 0.00390625
- vec_mom: float32 [5, 768], P(None, ('dp', 'seq')), may hold values from -0.00390625 to 0.00390625
- qkv_avg: float32 [2, 3, 768, 768], P(None, None, ('dp', 'seq')), may hold values from -0.21875 to 0.21875
- out_avg: float32 [2, 768, 768], P(None, ('dp', 'seq')), may hold values from -3.5 to 3.5
- up_avg: float32 [2, 768, 3072], P(None, ('dp', 'seq')), may hold values from -0.21875 to 0.21875
- down_avg: float32 [2, 3072, 768], P(None, ('dp', 'seq')), may hold values from -0.109375 to 0.109375
- vec_avg: float32 [5, 768], P(None, ('dp', 'seq')), may hold values from 0.5 to 1.5
Outputs:
- activations: bfloat16 [2048, 16, 768], P('seq', 'dp')
- input_grad: float32 [2048, 16, 768], P('seq', 'dp')
- grad_norm: float32 [], replicated
- qkv_new: float32 [2, 3, 768, 768], P(None, None, ('dp', 'seq'))
- out_new: float32 [2, 768, 768], P(None, ('dp', 'seq'))
- up_new: float32 [2, 768, 3072], P(None, ('dp', 'seq'))
- down_new: float32 [2, 3072, 768], P(None, ('dp', 'seq'))
- vec_new: float32 [5, 768], P(None, ('dp', 'seq'))
- qkv_mom_new: float32 [2, 3, 768, 768], P(None, None, ('dp', 'seq'))
- out_mom_new: float32 [2, 768, 768], P(None, ('dp', 'seq'))
- up_mom_new: float32 [2, 768, 3072], P(None, ('dp', 'seq'))
- down_mom_new: float32 [2, 3072, 768], P(None, ('dp', 'seq'))
- vec_mom_new: float32 [5, 768], P(None, ('dp', 'seq'))
- qkv_avg_new: float32 [2, 3, 768, 768], P(None, None, ('dp', 'seq'))
- out_avg_new: float32 [2, 768, 768], P(None, ('dp', 'seq'))
- up_avg_new: float32 [2, 768, 3072], P(None, ('dp', 'seq'))
- down_avg_new: float32 [2, 3072, 768], P(None, ('dp', 'seq'))
- vec_avg_new: float32 [5, 768], P(None, ('dp', 'seq'))
The draws below stay inside these ranges and needn't reach their ends.
Inputs may be any that keep to these rules, and one draw needn't show every extreme that they name: `lengths`: every length is 2048 or 1024, and both values occur. `picked_ids`: each sequence's 256 picks are distinct positions below its length, in rising order. `vectors`: rows 0, 1, 3, 4 are norm gains, row 2 the router's weight.
All inputs are finite; a program needn't handle non-finite values.
Results may differ from the reference program's by a relative error of at most 0.023.
Values may be sent and summed in bfloat16 or wider, within the bound.
No kernel may reach another device: no remote copies, remote signals or barrier semaphores. Data moves between devices by JAX's collectives and lax.ppermute only.
A program may use at most 256 MiB of HBM per device.

```python
import math
import jax
import jax.numpy as jnp
from jax import lax

D = 768
FF = 3072
HEADS = 12
HEAD = 64
LEN = 2048
CAP = 256
SEQS_ALL = 16
NPARAMS = 14159616


def draw_lengths_picks(key):
    count_all = SEQS_ALL
    coin_flip = jax.random.randint(jax.random.fold_in(key, 11), (count_all,), 0, 2)
    coin_flip = coin_flip.at[0].set(1).at[1].set(0)
    seq_lengths = jnp.where(coin_flip == 1, LEN, LEN // 2).astype(jnp.int32)
    order_keys = jax.random.split(jax.random.fold_in(key, 12), count_all)
    priority = jax.vmap(lambda one_key: jax.random.permutation(one_key, LEN))(order_keys).astype(jnp.int32)
    places = jnp.arange(LEN, dtype=jnp.int32)[None, :]
    priority = jnp.where(places < seq_lengths[:, None], priority, priority + LEN)
    priority = priority.at[0, LEN - 1].set(-1)
    chosen = jnp.argsort(priority, axis=1, stable=True)[:, :CAP]
    return (seq_lengths, jnp.sort(chosen, axis=1).astype(jnp.int32))


def draw_lengths(key, part):
    return draw_lengths_picks(key)[0]


def draw_picked_ids(key, part):
    return draw_lengths_picks(key)[1]


def draw_vectors(key, part):
    along = jnp.arange(D, dtype=jnp.float32)[None, :] / (D - 1)
    base_draw = jnp.clip(jax.random.normal(key, (5, D), jnp.float32), -4.0, 4.0)
    ramp = 0.6 * jnp.exp(along * math.log(3.0))
    gain_rows = ramp * (1.0 + 0.12 * base_draw)
    router_row = 0.75 / math.sqrt(D) * base_draw
    row_ids = jnp.arange(5)[:, None]
    return jnp.where(row_ids == 2, router_row, gain_rows)


def block_scale(own_key, dims, cuts, least, top_value):
    def one(position, blocks):
        draws = jax.random.uniform(jax.random.fold_in(jax.random.fold_in(own_key, 6), position), (blocks,), jnp.float32, least / len(cuts), top_value / len(cuts))
        return jnp.repeat(jnp.exp(draws), dims[position] // blocks).reshape((-1,) + (1,) * (len(dims) - position - 1))

    factor_of = one(*cuts[0])
    for cut in cuts[1:]:
        factor_of = factor_of * one(*cut)
    return factor_of


def centred(rng, shape, width, reach, cuts=(), kind=jnp.bfloat16):
    level = block_scale(rng, shape, cuts, -0.22, 0.18) if cuts else 1.0
    entries = jax.random.normal(rng, shape, jnp.float32) * width * level
    return jnp.minimum(jnp.maximum(entries, -reach), reach).astype(kind)


def setup_inputs(seed: int = 0) -> dict:
    splits = jax.random.split(jax.random.key(seed), 20)
    tokens = centred(splits[0], (LEN, SEQS_ALL, D), 1.0, 6.0, ((0, 8), (1, 4)))
    cotangent = centred(splits[1], (LEN, SEQS_ALL, D), 1.0, 6.0, ((0, 8), (1, 4)))
    picked_ids = draw_picked_ids(jax.random.fold_in(splits[19], 71), 0)
    lengths = draw_lengths(jax.random.fold_in(splits[19], 71), 0)
    qkv_w = centred(splits[4], (2, 3, D, D), D ** -0.5, 0.21875, ((2, 32),), jnp.float32)
    out_w = centred(splits[5], (2, D, D), (D * 8 // LEN) ** -0.5, 3.5, ((1, 32),), jnp.float32)
    up_w = centred(splits[6], (2, D, FF), D ** -0.5, 0.21875, ((1, 32),), jnp.float32)
    down_w = centred(splits[7], (2, FF, D), FF ** -0.5, 0.109375, ((1, 32),), jnp.float32)
    vectors = draw_vectors(jax.random.fold_in(splits[19], 71), 0)
    qkv_mom = centred(splits[9], (2, 3, D, D), (NPARAMS ** -0.5), 0.00390625, ((2, 32),), jnp.float32)
    out_mom = centred(splits[10], (2, D, D), (NPARAMS ** -0.5), 0.00390625, ((1, 32),), jnp.float32)
    up_mom = centred(splits[11], (2, D, FF), (NPARAMS ** -0.5), 0.00390625, ((1, 32),), jnp.float32)
    down_mom = centred(splits[12], (2, FF, D), (NPARAMS ** -0.5), 0.00390625, ((1, 32),), jnp.float32)
    vec_mom = centred(splits[13], (5, D), (NPARAMS ** -0.5), 0.00390625, ((1, 32),), jnp.float32)
    qkv_avg = centred(splits[14], (2, 3, D, D), D ** -0.5, 0.21875, ((2, 32),), jnp.float32)
    out_avg = centred(splits[15], (2, D, D), (D * 8 // LEN) ** -0.5, 3.5, ((1, 32),), jnp.float32)
    up_avg = centred(splits[16], (2, D, FF), D ** -0.5, 0.21875, ((1, 32),), jnp.float32)
    down_avg = centred(splits[17], (2, FF, D), FF ** -0.5, 0.109375, ((1, 32),), jnp.float32)
    vec_avg = jnp.clip(1.0 + 0.1 * jax.random.normal(splits[18], (5, D), jnp.float32), 0.5, 1.5)
    return {"tokens": tokens, "cotangent": cotangent, "picked_ids": picked_ids, "lengths": lengths, "qkv_w": qkv_w, "out_w": out_w, "up_w": up_w, "down_w": down_w, "vectors": vectors, "qkv_mom": qkv_mom, "out_mom": out_mom, "up_mom": up_mom, "down_mom": down_mom, "vec_mom": vec_mom, "qkv_avg": qkv_avg, "out_avg": out_avg, "up_avg": up_avg, "down_avg": down_avg, "vec_avg": vec_avg}


@jax.custom_vjp
def low(v):
    return lax.optimization_barrier(v.astype(jnp.bfloat16)).astype(jnp.float32)

@jax.custom_vjp
def low_back(v):
    return v

def low_keep(v):
    return (low(v), None)

def low_pass(kept, grad):
    return (grad,)

def back_keep(v):
    return (v, None)

def back_low(kept, grad):
    return (low(grad),)
low.defvjp(low_keep, low_pass)
low_back.defvjp(back_keep, back_low)
norm_eps = 1e-06
precise = lax.Precision.HIGHEST

def matmul(left, right):
    return jnp.dot(left, right, precision=precise)

def normed(value, gain):
    return value * lax.rsqrt(lax.optimization_barrier(jnp.mean(value * value, axis=-1, keepdims=True)) + norm_eps) * gain

def attention(query, keys_all, values_all, q_places, k_places, k_limit):
    row_count = query.shape[0]
    span_rows = min(512, row_count)
    heads_q = query.reshape(row_count // span_rows, span_rows, HEADS, HEAD)
    places = q_places.reshape(row_count // span_rows, span_rows)
    keys_h = keys_all.reshape(-1, HEADS, HEAD)
    values_h = values_all.reshape(-1, HEADS, HEAD)
    usable = k_places < k_limit

    def one_span(inputs):
        q_span, p_span = inputs
        scores = low_back(jnp.einsum('qha,kha->hqk', q_span, keys_h, precision=precise) * 0.125)
        allowed = (k_places[None, :] <= p_span[:, None]) & usable[None, :]
        scores = jnp.where(allowed[None], scores, -1e+30)
        weights = low(jax.nn.softmax(scores, axis=-1))
        return jnp.einsum('hqk,kha->qha', weights, values_h, precision=precise)
    mixed_out = lax.map(jax.checkpoint(one_span), (heads_q, places))
    return mixed_out.reshape(row_count, HEADS * HEAD)

def run_block(inputs_x, layer_id, params, gain_first, gain_second, q_places, k_places, k_limit):
    w_qkv, w_out, w_up, w_down = (params[0], params[1], params[2], params[3])
    first = low(normed(inputs_x, gain_first))
    query = low(low_back(matmul(first, w_qkv[layer_id, 0])))
    keys_all = low(low_back(matmul(first, w_qkv[layer_id, 1])))
    values_all = low(low_back(matmul(first, w_qkv[layer_id, 2])))
    attended = low(low_back(attention(query, keys_all, values_all, q_places, k_places, k_limit)))
    branch = low_back(matmul(attended, w_out[layer_id]))
    middle = inputs_x + branch
    second = low(normed(middle, gain_second))
    pre_act = low_back(matmul(second, w_up[layer_id]))
    act_out = low(jax.nn.gelu(pre_act))
    mlp_out = low_back(matmul(act_out, w_down[layer_id]))
    return (branch, middle, mlp_out)

def one_sequence(params, sequence, picked, length):
    w_vec = params[4]
    places = jnp.arange(LEN, dtype=jnp.int32)
    chosen = sequence[picked]
    gate = jax.nn.sigmoid(matmul(chosen, w_vec[2]))
    branch, middle, mlp_out = run_block(chosen, 0, params, w_vec[0], w_vec[1], picked, picked, length)
    delta = low(gate[:, None] * (branch + mlp_out))
    mixed_in = sequence.at[picked].add(delta)
    branch_d, middle_d, mlp_d = run_block(mixed_in, 1, params, w_vec[3], w_vec[4], places, places, length)
    live = (places < length).astype(jnp.float32)
    return live[:, None] * (middle_d + mlp_d)

def reference(tokens, cotangent, picked_ids, lengths, qkv_w, out_w, up_w, down_w, vectors, qkv_mom, out_mom, up_mom, down_mom, vec_mom, qkv_avg, out_avg, up_avg, down_avg, vec_avg):
    masters = (qkv_w, out_w, up_w, down_w, vectors)
    inputs_seq = jnp.swapaxes(tokens.astype(jnp.float32), 0, 1)

    def forward(weights_in, sequences):
        rounded = tuple((low(element) for element in weights_in))

        def step_fn(carry_in, entry_in):
            return (carry_in, jax.checkpoint(one_sequence)(rounded, entry_in[0], entry_in[1], entry_in[2]))
        _, outputs = lax.scan(step_fn, jnp.zeros((), jnp.float32), (sequences, picked_ids, lengths))
        return outputs
    outputs, pullback = jax.vjp(forward, masters, inputs_seq)
    grads, seq_grad = pullback(jnp.swapaxes(cotangent.astype(jnp.float32), 0, 1))
    squares = sum((jnp.sum(piece * piece) for piece in grads))
    grad_norm = jnp.sqrt(squares)
    factor = 1.0 / jnp.maximum(grad_norm, 1.0)
    base_rate = math.sqrt(NPARAMS / D)
    rates = (base_rate, math.sqrt(NPARAMS * LEN / (8 * D)), base_rate, base_rate, base_rate)
    moms = (qkv_mom, out_mom, up_mom, down_mom, vec_mom)
    avgs = (qkv_avg, out_avg, up_avg, down_avg, vec_avg)
    new_weights = []
    new_moms = []
    new_avgs = []
    for weight, gradient, momentum, average, rate in zip(masters, grads, moms, avgs, rates):
        clipped = gradient * factor
        momentum_new = 0.5 * momentum + clipped
        weight_new = weight - rate * (clipped + 0.5 * momentum_new)
        new_weights.append(weight_new)
        new_moms.append(momentum_new)
        new_avgs.append(0.5 * average + 0.5 * weight_new)
    activations = jnp.swapaxes(outputs, 0, 1).astype(jnp.bfloat16)
    input_grad = jnp.swapaxes(seq_grad, 0, 1)
    return (activations, input_grad, grad_norm, new_weights[0], new_weights[1], new_weights[2], new_weights[3], new_weights[4], new_moms[0], new_moms[1], new_moms[2], new_moms[3], new_moms[4], new_avgs[0], new_avgs[1], new_avgs[2], new_avgs[3], new_avgs[4])
```

```python
import functools
import math

import jax
import jax.numpy as jnp
from jax import lax
from jax.experimental import pallas as pl
from jax.experimental.pallas import tpu as pltpu
from jax.sharding import Mesh
from jax.sharding import PartitionSpec as P

D = 768
FF = 3072
LEN = 2048
NPARAMS = 14159616
EPS = 1e-06
PAIRS = 6
TQ = 256
NN = (((1,), (0,)), ((), ()))
NT = (((1,), (1,)), ((), ()))
TN = (((0,), (0,)), ((), ()))
BF = jnp.bfloat16
F32 = jnp.float32


def dotf(left, right, dims):
    return lax.dot_general(left, right, dims, preferred_element_type=F32)


def far_mask(core, tile, lb, q_axis):
    shift = lb.bit_length() - 1
    iq = lax.broadcasted_iota(jnp.int32, (TQ, TQ), q_axis) >> shift
    ik = lax.broadcasted_iota(jnp.int32, (TQ, TQ), 1 - q_axis) >> shift
    odd = (core + tile * (TQ >> shift) + iq) & 1
    return (iq > ik) | ((iq == ik) & (odd == 1))


def attend_kernel(lb, core_ref, *refs):
    if lb:
        q_ref, ko, vo, kf, vf, o_ref, lse_ref = refs
    else:
        q_ref, ko, vo, o_ref, lse_ref = refs
    rows = q_ref.shape[0]
    lane = lax.broadcasted_iota(jnp.int32, (TQ, 128), 1)
    tri = lax.broadcasted_iota(jnp.int32, (TQ, TQ), 0) >= lax.broadcasted_iota(
        jnp.int32, (TQ, TQ), 1
    )
    for t in range(rows // TQ):
        n = t * TQ
        q = q_ref[pl.ds(n, TQ), :] * BF(0.125)
        outs = []
        cols = []
        if lb:
            fm = far_mask(core_ref[0], t, lb, 0)
        for h in range(2):
            qm = jnp.where((lane >= 64) if h else (lane < 64), q, BF(0))
            segs = []
            if t:
                segs.append((dotf(qm, ko[pl.ds(0, n), :], NT), vo[pl.ds(0, n), :]))
            segs.append(
                (jnp.where(tri, dotf(qm, ko[pl.ds(n, TQ), :], NT), -1e30), vo[pl.ds(n, TQ), :])
            )
            if lb:
                if t:
                    segs.append((dotf(qm, kf[pl.ds(0, n), :], NT), vf[pl.ds(0, n), :]))
                segs.append(
                    (jnp.where(fm, dotf(qm, kf[pl.ds(n, TQ), :], NT), -1e30), vf[pl.ds(n, TQ), :])
                )
            top = functools.reduce(
                jnp.maximum, [jnp.max(s, axis=1, keepdims=True) for s, _ in segs]
            )
            total = 0.0
            acc = 0.0
            for s, v in segs:
                e = jnp.exp(s - top)
                total = total + jnp.sum(e, axis=1, keepdims=True)
                acc = acc + dotf(e.astype(BF), v, NN)
            outs.append(acc * (1.0 / total))
            cols.append(jnp.broadcast_to(top + jnp.log(total), (TQ, 128)))
        o_ref[pl.ds(n, TQ), :] = jnp.where(lane < 64, outs[0], outs[1]).astype(BF)
        for h in range(2):
            lse_ref[0, pl.ds(h, 1), pl.ds(n, TQ)] = cols[h].T[0:1, :]


def attend(q, k_own, v_own, far, core, lb):
    rows = q[0].shape[0]
    ops = [q, k_own, v_own] + list(far)

    def spec(off):
        return pl.BlockSpec((rows, 128), lambda i, off=off: (0, off + i))

    size = 12 * rows * rows * (1 if far else 0.5)
    return pl.pallas_call(
        functools.partial(attend_kernel, lb if far else 0),
        grid=(PAIRS,),
        in_specs=[pl.BlockSpec(memory_space=pltpu.SMEM)] + [spec(o) for _, o in ops],
        out_specs=[spec(0), pl.BlockSpec((1, 2, rows), lambda i: (i, 0, 0))],
        out_shape=[
            jax.ShapeDtypeStruct((rows, D), BF),
            jax.ShapeDtypeStruct((PAIRS, 2, rows), F32),
        ],
        compiler_params=pltpu.CompilerParams(vmem_limit_bytes=40 * 2**20),
        cost_estimate=pl.CostEstimate(
            flops=int(4 * 64 * 6 * size), bytes_accessed=rows * D * 12, transcendentals=int(size)
        ),
        name="attend_far" if far else "attend_own",
    )(core, *[a for a, _ in ops])


def attend_back_kernel(lb, kc, core_ref, *refs):
    if lb:
        q_ref, do_ref, o_ref, lse_ref, ko, vo, kf, vf = refs[:8]
        dq_ref, dko, dvo, dkf, dvf, k_t, aok, aov, afk, afv = refs[8:]
        parts = [(ko, vo, aok, aov, 0), (kf, vf, afk, afv, 1)]
    else:
        q_ref, do_ref, o_ref, lse_ref, ko, vo, dq_ref, dko, dvo, k_t, aok, aov = refs
        parts = [(ko, vo, aok, aov, 0)]
    rows = q_ref.shape[0]
    lane = lax.broadcasted_iota(jnp.int32, (TQ, 128), 1)
    tri = lax.broadcasted_iota(jnp.int32, (TQ, TQ), 1) >= lax.broadcasted_iota(
        jnp.int32, (TQ, TQ), 0
    )
    for k, _, ak, av, s in parts:
        k_t[s] = k[...].astype(F32).T.astype(BF)
        ak[...] = jnp.zeros_like(ak)
        av[...] = jnp.zeros_like(av)
    for t in range(rows // TQ):
        n = t * TQ
        q = q_ref[pl.ds(n, TQ), :] * BF(0.125)
        do = do_ref[pl.ds(n, TQ), :]
        prod = (do.astype(F32) * o_ref[pl.ds(n, TQ), :].astype(F32)).T
        dqs = []
        if lb:
            fm = far_mask(core_ref[0], t, lb, 1)
        for h in range(2):
            half = (lane >= 64) if h else (lane < 64)
            qm = jnp.where(half, q, BF(0))
            dom = jnp.where(half, do, BF(0))
            inner = jnp.sum(prod[64 * h : 64 * h + 64], axis=0, keepdims=True)
            lse = lse_ref[0, pl.ds(h, 1), pl.ds(n, TQ)]
            dq_t = 0.0
            for k, v, ak, av, s in parts:
                spans = []
                a = 0
                while a < n:
                    w = min(kc, n - a)
                    spans.append((a, w, None))
                    a += w
                spans.append((n, TQ, fm if s else tri))
                for a, w, mask in spans:
                    p = jnp.exp(dotf(k[pl.ds(a, w), :], qm, NT) - lse)
                    if mask is not None:
                        p = jnp.where(mask, p, 0.0)
                    dp = dotf(v[pl.ds(a, w), :], dom, NT)
                    ds = (p * (dp - inner)).astype(BF)
                    av[pl.ds(a, w), :] += dotf(p.astype(BF), dom, NN)
                    ak[pl.ds(a, w), :] += dotf(ds, qm, NN)
                    dq_t = dq_t + dotf(k_t[s, 64 * h : 64 * h + 64, a : a + w], ds, NN)
            dqs.append(dq_t)
        dq_ref[pl.ds(n, TQ), :] = (jnp.concatenate(dqs, axis=0) * 0.125).T.astype(BF)
    dko[...] = aok[...].astype(dko.dtype)
    dvo[...] = aov[...].astype(dvo.dtype)
    if lb:
        dkf[...] = afk[...].astype(dkf.dtype)
        dvf[...] = afv[...].astype(dvf.dtype)


def attend_back(q, do, o, lse, k_own, v_own, far, core, lb, own_type, kc=512):
    rows = do[0].shape[0]

    def spec(off):
        return pl.BlockSpec((rows, 128), lambda i, off=off: (0, off + i))

    lse_spec = pl.BlockSpec((1, 2, rows), lambda i: (i, 0, 0))
    ops = [q, do, o, None, k_own, v_own] + list(far)
    types = [BF, own_type, own_type] + ([BF] * 2 if far else [])
    size = 12 * rows * rows * (1 if far else 0.5)
    return pl.pallas_call(
        functools.partial(attend_back_kernel, lb if far else 0, kc),
        grid=(PAIRS,),
        in_specs=[pl.BlockSpec(memory_space=pltpu.SMEM)]
        + [lse_spec if e is None else spec(e[1]) for e in ops],
        out_specs=[spec(0)] * len(types),
        out_shape=[jax.ShapeDtypeStruct((rows, D), t) for t in types],
        scratch_shapes=[pltpu.VMEM((2 if far else 1, 128, rows), BF)]
        + [pltpu.VMEM((rows, 128), F32)] * (len(types) - 1),
        compiler_params=pltpu.CompilerParams(vmem_limit_bytes=40 * 2**20),
        cost_estimate=pl.CostEstimate(
            flops=int(10 * 64 * 5 * size), bytes_accessed=rows * D * 24, transcendentals=int(size)
        ),
        name="attend_back_far" if far else "attend_back_own",
    )(core, *[lse if e is None else e[0] for e in ops])


def norm_parts(rows):
    scale = lax.rsqrt(jnp.mean(rows * rows, axis=-1, keepdims=True) + EPS)
    return rows * scale, scale


def norm_back(d_out, unit, scale, gain):
    d_gain = jnp.sum(d_out * unit, axis=0)
    d_unit = d_out * gain
    d_rows = scale * (d_unit - unit * jnp.mean(d_unit * unit, axis=-1, keepdims=True))
    return d_rows, d_gain


def gelu_parts(pre):
    c = math.sqrt(2.0 / math.pi)
    sq = pre * pre
    t = jnp.tanh(c * pre * (1.0 + 0.044715 * sq))
    act = 0.5 * pre * (1.0 + t)
    slope = 0.5 * (1.0 + t) + 0.5 * pre * (1.0 - t * t) * (c * (1.0 + 3 * 0.044715 * sq))
    return act.astype(BF), slope.astype(BF)


def block_forward(rows, weights, gain_a, gain_b, far_of, core, lb):
    w_qkv, w_out, w_up, w_down = weights
    unit_a, scale_a = norm_parts(rows)
    n1 = (unit_a * gain_a).astype(BF)
    qkv = dotf(n1, w_qkv, NN).astype(BF)
    far = far_of(qkv)
    own = ((qkv, 0), (qkv, 6), (qkv, 12))
    o, lse = attend(*own, far, core, lb)
    branch = dotf(o, w_out, NN)
    mid = rows + branch
    unit_b, scale_b = norm_parts(mid)
    n2 = (unit_b * gain_b).astype(BF)
    act, slope = gelu_parts(dotf(n2, w_up, NN))
    mlp = dotf(act, w_down, NN)
    return branch, mid, mlp, (n1, own, far, o, lse, n2, act, slope)


def block_backward(
    rows, mid, weights, gain_a, gain_b, saved, d_mlp, d_top, d_extra, home, pick, core, lb
):
    w_qkv, w_out, w_up, w_down = weights
    n1, own, far, o, lse, n2, act, slope = saved
    mlp_low = d_mlp.astype(BF)
    g_down = dotf(pick(act), mlp_low, TN).astype(BF)
    d_pre = (slope.astype(F32) * dotf(mlp_low, w_down, NT)).astype(BF)
    g_up = dotf(pick(n2), d_pre, TN).astype(BF)
    unit_b, scale_b = norm_parts(mid)
    d_mid, g_b = norm_back(dotf(d_pre, w_up, NT), unit_b, scale_b, gain_b)
    if d_top is not None:
        d_mid = d_mid + d_top
    d_branch = (d_mid if d_extra is None else d_mid + d_extra).astype(BF)
    g_out = dotf(pick(o), d_branch, TN).astype(BF)
    do = dotf(d_branch, w_out, NT).astype(BF)
    back = attend_back(own[0], (do, 0), (o, 0), lse, own[1], own[2], far, core, lb, F32 if far else BF)
    d_qkv = jnp.concatenate([back[0]] + home(back[1:]), axis=1)
    g_qkv = dotf(pick(n1), d_qkv, TN).astype(BF)
    unit_a, scale_a = norm_parts(rows)
    d_rows, g_a = norm_back(dotf(d_qkv, w_qkv, NT), unit_a, scale_a, gain_a)
    return d_rows + d_mid, (g_qkv, g_out, g_up, g_down), g_a, g_b


def shifted(value, axes, sizes, steps):
    pairs = []
    total = math.prod(sizes)
    for source in range(total):
        rest = source
        place = []
        for size in reversed(sizes):
            place.append(rest % size)
            rest //= size
        target = 0
        for size, at, step in zip(sizes, reversed(place), steps):
            target = target * size + (at + step) % size
        pairs.append((source, target))
    return lax.ppermute(value, axes, pairs)


def solution(mesh):
    dp, seq = mesh.shape["dp"], mesh.shape["seq"]
    y_n = dp // 2
    x_n = y_n if seq % y_n == 0 else 1
    z_n = seq // x_n
    half = seq // 2
    ways = dp * seq
    inner = Mesh(mesh.devices.reshape(y_n, 2, z_n, x_n), ("y", "core", "z", "x"))
    every = ("y", "core", "z", "x")
    home_axes = ("core", "z", "x")
    lb = LEN // seq

    def route(t):
        pairs = []
        for c in range(2):
            for s in range(seq):
                block = s // 2
                core = (s ^ block) & 1
                pairs.append((c * seq + s, core * seq + 2 * ((block + t) % half) + c))
        return pairs

    routes = [route(t) for t in range(half)]

    def swap_core(value):
        return lax.ppermute(value, "core", [(0, 1), (1, 0)])

    def all_sum(value):
        for axis, size in (("core", 2), ("x", x_n), ("y", y_n), ("z", z_n)):
            value = sum(
                (shifted(value, (axis,), (size,), (s,)) for s in range(1, size)), start=value
            )
        return value

    def body(
        tokens, cotangent, picked_ids, lengths,
        qkv_w, out_w, up_w, down_w, vectors,
        qkv_mom, out_mom, up_mom, down_mom, vec_mom,
        qkv_avg, out_avg, up_avg, down_avg, vec_avg,
    ):
        y, core, z, x = (lax.axis_index(a) for a in every)
        chip = z * x_n + x
        seq_id = chip // 2
        group = chip % 2
        core_arr = jnp.full((1,), core, jnp.int32)
        piece = D // ways

        def grown(value, axis, size, place, dim):
            if size == 1:
                return jnp.expand_dims(value, dim)
            behind = [shifted(value, (axis,), (size,), (s,)) for s in range(1, size)]
            if size == 2:
                first = place == 0
                return jnp.stack(
                    [jnp.where(first, value, behind[0]), jnp.where(first, behind[0], value)], dim
                )
            twice = jnp.stack(([value] + behind[::-1]) * 2, dim)
            return lax.dynamic_slice_in_dim(twice, size - place, size, dim)

        def spread(shard, x_first):
            value = grown(shard, "z", z_n, z, 0)
            if x_first:
                value = grown(value, "x", x_n, x, 1)
                value = grown(value, "y", y_n, y, 0)
            else:
                value = grown(value, "y", y_n, y, 0)
                value = grown(value, "x", x_n, x, 2)
            value = grown(value, "core", 2, core, 1)
            return value.reshape(ways * shard.shape[0], shard.shape[1])

        shard_a = jnp.concatenate(
            [qkv_w[0].transpose(1, 0, 2).reshape(piece, 3 * D), out_w[0]], axis=1
        ).astype(BF)
        gains_row = jnp.pad(vectors.T, ((0, 0), (0, 128 - 5))).astype(BF)
        full_a = spread(jnp.concatenate([shard_a, gains_row], axis=1), True)
        gains = full_a[:, 4 * D : 4 * D + 5].T.astype(F32)
        weights0 = (
            full_a[:, : 3 * D],
            full_a[:, 3 * D : 4 * D],
            spread(up_w[0].astype(BF), False),
            spread(down_w[0].astype(BF), True),
        )

        packed = jnp.concatenate(
            [
                qkv_w[1].reshape(3 * piece, D),
                out_w[1],
                up_w[1].reshape(piece, 4, D).transpose(1, 0, 2).reshape(4 * piece, D),
                down_w[1],
            ]
        ).astype(BF)
        full = lax.all_gather(packed, every, axis=0, tiled=False)
        w_qkv = full[:, : 3 * piece].reshape(ways, 3, piece, D).transpose(0, 2, 1, 3)
        w_out = full[:, 3 * piece : 4 * piece]
        w_up = full[:, 4 * piece : 8 * piece].reshape(ways, 4, piece, D).transpose(0, 2, 1, 3)
        w_down = full[:, 8 * piece :]
        weights1 = (
            w_qkv.reshape(D, 3 * D),
            w_out.reshape(D, D),
            w_up.reshape(D, FF),
            w_down.reshape(FF, D),
        )

        def rolled(parts, start):
            count = len(parts)
            twice = jnp.stack(parts + parts)
            return lax.dynamic_slice_in_dim(twice, (count - start) % count, count, 0)

        def come(source):
            by_seq = source.transpose(1, 0, 2)
            got = []
            for t in range(half):
                sent = lax.dynamic_index_in_dim(by_seq, (chip // 2 + t) % half, 0, keepdims=False)
                got.append(lax.ppermute(sent, home_axes, routes[t]))
            return rolled(got[:1] + got[:0:-1], seq_id).reshape(half * lb, D)

        def leave(rows):
            got = []
            for t in range(half):
                sent = lax.dynamic_slice(rows, (((seq_id - t) % half) * lb, 0), (lb, D))
                got.append(lax.ppermute(sent, home_axes, [(b, a) for a, b in routes[t]]))
            return rolled(got, chip // 2).transpose(1, 0, 2)

        own_x = come(tokens)
        own_cot = come(cotangent)
        meta = jnp.concatenate([picked_ids, lengths[:, None]], axis=1)
        meta = lax.dynamic_index_in_dim(
            jnp.where(group == core, meta, swap_core(meta)), seq_id, 0, keepdims=False
        )
        picks, length = meta[:-1], meta[-1]
        row_ids = jnp.arange(half * lb, dtype=jnp.int32)
        block = row_ids // lb
        places = (2 * block + ((core + block) & 1)) * lb + row_ids % lb
        chosen = (picks[:, None] == places[None, :]).astype(BF)
        live = (places < length).astype(F32)[:, None]

        def at_picks(rows):
            part = dotf(chosen, rows, NN).astype(BF)
            return part + swap_core(part)

        def to_rows(values):
            return dotf(chosen, values, TN)

        x_low = at_picks(own_x)
        x_rows = x_low.astype(F32)
        gate = jax.nn.sigmoid(jnp.sum(x_rows * gains[2], axis=-1, keepdims=True))
        branch0, mid0, mlp0, saved0 = block_forward(
            x_rows, weights0, gains[0], gains[1], lambda qkv: (), core_arr, lb
        )
        both0 = branch0 + mlp0
        delta = (gate * both0).astype(BF)
        mixed = own_x.astype(F32) + to_rows(delta)

        def far_of(qkv):
            far = swap_core(qkv[:, D:])
            return ((far, 0), (far, 6))

        def home1(parts):
            dk, dv, dk_far, dv_far = parts
            back = swap_core(jnp.concatenate([dk_far, dv_far], axis=1)).astype(F32)
            return [(dk + back[:, :D]).astype(BF), (dv + back[:, D:]).astype(BF)]

        branch1, mid1, mlp1, saved1 = block_forward(
            mixed, weights1, gains[3], gains[4], far_of, core_arr, lb
        )
        activations = leave((live * (mid1 + mlp1)).astype(BF))
        d_top = live * own_cot.astype(F32)
        d_mixed, grads1, g_a1, g_b1 = block_backward(
            mixed, mid1, weights1, gains[3], gains[4], saved1, d_top, d_top, None,
            home1, lambda a: a, core_arr, lb,
        )

        def mine(rows):
            width = rows.shape[1]
            split = rows.reshape(rows.shape[0], y_n, 2, width // dp)
            return lax.dynamic_index_in_dim(split, core, 2, keepdims=False).reshape(
                rows.shape[0], width // 2
            )

        d_delta = at_picks(d_mixed.astype(BF)).astype(F32)
        gated = gate * d_delta
        d_logit = gate * (1.0 - gate) * jnp.sum(d_delta * both0, axis=-1, keepdims=True)
        d_rows0, grads0, g_a0, g_b0 = block_backward(
            x_rows, mid0, weights0, gains[0], gains[1], saved0, gated, None, gated,
            lambda parts: list(parts), mine, core_arr, lb,
        )
        g_r = jnp.sum(d_logit * x_rows, axis=0)
        d_chosen = (d_rows0 + d_logit * gains[2]).astype(BF)
        input_grad = leave((d_mixed + to_rows(d_chosen)).astype(BF)).astype(F32)

        def packed_rows(grad, which):
            cores = 1 if which is None else 2
            block = grad.shape[0] * grad.shape[1] // (y_n * cores * z_n * x_n * D)
            wide = grad.shape[1] // D
            split = grad.reshape(y_n, cores, z_n, x_n, block // wide, wide, D)
            if which is None:
                split = split[:, 0]
            else:
                split = lax.dynamic_index_in_dim(split, which, 1, keepdims=False)
            return jnp.swapaxes(split, 3, 4).reshape(y_n, z_n, x_n, block, D)

        def pack(grads, which):
            return jnp.concatenate([packed_rows(g, which) for g in grads], axis=3)

        def over_core(grads):
            got = swap_core(pack(grads, 1 - core))
            return (pack(grads, core).astype(F32) + got.astype(F32)).astype(BF)

        def over(value, axis, size, place, dim, kind=BF):
            total = lax.dynamic_index_in_dim(value, place, dim, keepdims=False).astype(F32)
            for s in range(1, size):
                sent = lax.dynamic_index_in_dim(value, (place + s) % size, dim, keepdims=False)
                total = total + shifted(sent, (axis,), (size,), (s,)).astype(F32)
            return total.astype(kind)

        def over_chips(value):
            cut = value.shape[3] // 16 * 8
            one = over(over(value[..., :cut, :], "y", y_n, y, 0), "x", x_n, x, 1)
            two = over(over(value[..., cut:, :], "x", x_n, x, 2), "y", y_n, y, 0)
            return over(jnp.concatenate([one, two], axis=1), "z", z_n, z, 0, F32)

        tail1 = lax.psum_scatter(
            over_core(grads1[1:]).reshape(ways // 2, 9 * piece, D),
            ("y", "z", "x"), scatter_dimension=0,
        ).astype(F32)
        head1 = over_chips(over_core(grads1[:1]))
        tail0 = over_chips(pack(grads0[1:], None))
        head0 = over_chips(pack(grads0[:1], None))
        g_vec = all_sum(jnp.stack([0.5 * g_a0, 0.5 * g_b0, 0.5 * g_r, g_a1, g_b1]))
        shard_id = ((y * 2 + core) * z_n + z) * x_n + x
        both = ((head0, tail0), (head1, tail1))
        shards = [
            jnp.stack([h.reshape(3, piece, D) for h, _ in both]),
            jnp.stack([t[:piece] for _, t in both]),
            jnp.stack(
                [
                    t[piece : 5 * piece].reshape(4, piece, D).transpose(1, 0, 2).reshape(piece, FF)
                    for _, t in both
                ]
            ),
            jnp.stack([t[5 * piece :] for _, t in both]),
        ]
        squares = sum(jnp.sum(s * s) for s in shards)
        norm_sq = all_sum(squares.reshape(1, 1))[0, 0] + jnp.sum(g_vec * g_vec)
        grad_norm = jnp.sqrt(norm_sq)
        shards.append(lax.dynamic_slice(g_vec, (0, shard_id * piece), (5, piece)))
        factor = 1.0 / jnp.maximum(grad_norm, 1.0)
        base_rate = math.sqrt(NPARAMS / D)
        rates = (base_rate, math.sqrt(NPARAMS * LEN / (8 * D)), base_rate, base_rate, base_rate)
        masters = (qkv_w, out_w, up_w, down_w, vectors)
        moms = (qkv_mom, out_mom, up_mom, down_mom, vec_mom)
        avgs = (qkv_avg, out_avg, up_avg, down_avg, vec_avg)
        new_w, new_m, new_z = [], [], []
        for weight, grad, mom, avg, rate in zip(masters, shards, moms, avgs, rates):
            clipped = grad * factor
            m = 0.5 * mom + clipped
            w = weight - rate * (clipped + 0.5 * m)
            new_w.append(w)
            new_m.append(m)
            new_z.append(0.5 * avg + 0.5 * w)
        return (activations, input_grad, grad_norm, *new_w, *new_m, *new_z)

    group_spec = ("y", "core")
    pos_spec = ("z", "x")
    rows_spec = P(pos_spec, group_spec, None)
    param_specs = (
        P(None, None, every, None),
        P(None, every, None),
        P(None, every, None),
        P(None, every, None),
        P(None, every),
    )
    return jax.shard_map(
        body,
        mesh=inner,
        in_specs=(rows_spec, rows_spec, P(group_spec, None), P(group_spec)) + param_specs * 3,
        out_specs=(rows_spec, rows_spec, P()) + param_specs * 3,
        check_vma=False,
    )
```

```python
import functools
import math

import jax
import jax.numpy as jnp
from jax import lax
from jax.experimental import pallas as pl
from jax.experimental.pallas import tpu as pltpu
from jax.sharding import Mesh
from jax.sharding import PartitionSpec as P

D = 768
FF = 3072
LEN = 2048
NPARAMS = 14159616
EPS = 1e-06
PAIRS = 6
TQ = 256
NN = (((1,), (0,)), ((), ()))
NT = (((1,), (1,)), ((), ()))
TN = (((0,), (0,)), ((), ()))
BF = jnp.bfloat16
F32 = jnp.float32


def dotf(left, right, dims):
    return lax.dot_general(left, right, dims, preferred_element_type=F32)


def far_mask(core, tile, lb, q_axis):
    shift = lb.bit_length() - 1
    iq = lax.broadcasted_iota(jnp.int32, (TQ, TQ), q_axis) >> shift
    ik = lax.broadcasted_iota(jnp.int32, (TQ, TQ), 1 - q_axis) >> shift
    odd = (core + tile * (TQ >> shift) + iq) & 1
    return (iq > ik) | ((iq == ik) & (odd == 1))


def attend_kernel(lb, core_ref, *refs):
    if lb:
        q_ref, ko, vo, kf, vf, o_ref, lse_ref = refs
    else:
        q_ref, ko, vo, o_ref, lse_ref = refs
    rows = q_ref.shape[0]
    lane = lax.broadcasted_iota(jnp.int32, (TQ, 128), 1)
    tri = lax.broadcasted_iota(jnp.int32, (TQ, TQ), 0) >= lax.broadcasted_iota(
        jnp.int32, (TQ, TQ), 1
    )
    for t in range(rows // TQ):
        n = t * TQ
        q = q_ref[pl.ds(n, TQ), :] * BF(0.125)
        outs = []
        cols = []
        if lb:
            fm = far_mask(core_ref[0], t, lb, 0)
        for h in range(2):
            qm = jnp.where((lane >= 64) if h else (lane < 64), q, BF(0))
            segs = []
            if t:
                segs.append((dotf(qm, ko[pl.ds(0, n), :], NT), vo[pl.ds(0, n), :]))
            segs.append(
                (jnp.where(tri, dotf(qm, ko[pl.ds(n, TQ), :], NT), -1e30), vo[pl.ds(n, TQ), :])
            )
            if lb:
                if t:
                    segs.append((dotf(qm, kf[pl.ds(0, n), :], NT), vf[pl.ds(0, n), :]))
                segs.append(
                    (jnp.where(fm, dotf(qm, kf[pl.ds(n, TQ), :], NT), -1e30), vf[pl.ds(n, TQ), :])
                )
            top = functools.reduce(
                jnp.maximum, [jnp.max(s, axis=1, keepdims=True) for s, _ in segs]
            )
            total = 0.0
            acc = 0.0
            for s, v in segs:
                e = jnp.exp(s - top)
                total = total + jnp.sum(e, axis=1, keepdims=True)
                acc = acc + dotf(e.astype(BF), v, NN)
            outs.append(acc * (1.0 / total))
            cols.append(jnp.broadcast_to(top + jnp.log(total), (TQ, 128)))
        o_ref[pl.ds(n, TQ), :] = jnp.where(lane < 64, outs[0], outs[1]).astype(BF)
        for h in range(2):
            lse_ref[0, pl.ds(h, 1), pl.ds(n, TQ)] = cols[h].T[0:1, :]


def attend(q, k_own, v_own, far, core, lb):
    rows = q[0].shape[0]
    ops = [q, k_own, v_own] + list(far)

    def spec(off):
        return pl.BlockSpec((rows, 128), lambda i, off=off: (0, off + i))

    size = 12 * rows * rows * (1 if far else 0.5)
    return pl.pallas_call(
        functools.partial(attend_kernel, lb if far else 0),
        grid=(PAIRS,),
        in_specs=[pl.BlockSpec(memory_space=pltpu.SMEM)] + [spec(o) for _, o in ops],
        out_specs=[spec(0), pl.BlockSpec((1, 2, rows), lambda i: (i, 0, 0))],
        out_shape=[
            jax.ShapeDtypeStruct((rows, D), BF),
            jax.ShapeDtypeStruct((PAIRS, 2, rows), F32),
        ],
        compiler_params=pltpu.CompilerParams(vmem_limit_bytes=40 * 2**20),
        cost_estimate=pl.CostEstimate(
            flops=int(4 * 64 * 6 * size), bytes_accessed=rows * D * 12, transcendentals=int(size)
        ),
        name="attend_far" if far else "attend_own",
    )(core, *[a for a, _ in ops])


def attend_back_kernel(lb, kc, core_ref, *refs):
    if lb:
        q_ref, do_ref, o_ref, lse_ref, ko, vo, kf, vf = refs[:8]
        dq_ref, d_own, d_far, k_t, aok, aov, afk, afv = refs[8:]
        parts = [(ko, vo, aok, aov, 0), (kf, vf, afk, afv, 1)]
    else:
        q_ref, do_ref, o_ref, lse_ref, ko, vo, dq_ref, d_own, k_t, aok, aov = refs
        parts = [(ko, vo, aok, aov, 0)]
    rows = q_ref.shape[0]
    lane = lax.broadcasted_iota(jnp.int32, (TQ, 128), 1)
    tri = lax.broadcasted_iota(jnp.int32, (TQ, TQ), 1) >= lax.broadcasted_iota(
        jnp.int32, (TQ, TQ), 0
    )
    for k, _, ak, av, s in parts:
        k_t[s] = k[...].astype(F32).T.astype(BF)
        ak[...] = jnp.zeros_like(ak)
        av[...] = jnp.zeros_like(av)
    for t in range(rows // TQ):
        n = t * TQ
        q = q_ref[pl.ds(n, TQ), :] * BF(0.125)
        do = do_ref[pl.ds(n, TQ), :]
        prod = (do.astype(F32) * o_ref[pl.ds(n, TQ), :].astype(F32)).T
        dqs = []
        if lb:
            fm = far_mask(core_ref[0], t, lb, 1)
        for h in range(2):
            half = (lane >= 64) if h else (lane < 64)
            qm = jnp.where(half, q, BF(0))
            dom = jnp.where(half, do, BF(0))
            inner = jnp.sum(prod[64 * h : 64 * h + 64], axis=0, keepdims=True)
            lse = lse_ref[0, pl.ds(h, 1), pl.ds(n, TQ)]
            dq_t = 0.0
            for k, v, ak, av, s in parts:
                spans = []
                a = 0
                while a < n:
                    w = min(kc, n - a)
                    spans.append((a, w, None))
                    a += w
                spans.append((n, TQ, fm if s else tri))
                for a, w, mask in spans:
                    p = jnp.exp(dotf(k[pl.ds(a, w), :], qm, NT) - lse)
                    if mask is not None:
                        p = jnp.where(mask, p, 0.0)
                    dp = dotf(v[pl.ds(a, w), :], dom, NT)
                    ds = (p * (dp - inner)).astype(BF)
                    av[pl.ds(a, w), :] += dotf(p.astype(BF), dom, NN)
                    ak[pl.ds(a, w), :] += dotf(ds, qm, NN)
                    dq_t = dq_t + dotf(k_t[s, 64 * h : 64 * h + 64, a : a + w], ds, NN)
            dqs.append(dq_t)
        dq_ref[pl.ds(n, TQ), :] = (jnp.concatenate(dqs, axis=0) * 0.125).T.astype(BF)
    d_own[0] = aok[...].astype(d_own.dtype)
    d_own[1] = aov[...].astype(d_own.dtype)
    if lb:
        d_far[0] = afk[...].astype(BF)
        d_far[1] = afv[...].astype(BF)


def attend_back(q, do, o, lse, k_own, v_own, far, core, lb, first, count, kc=512):
    rows = do[0].shape[0]

    def spec(off):
        return pl.BlockSpec((rows, 128), lambda i, off=off: (0, off + i))

    two = pl.BlockSpec((2, rows, 128), lambda i: (0, 0, i))
    lse_spec = pl.BlockSpec((1, 2, rows), lambda i: (i + first, 0, 0))
    ops = [q, do, o, None, k_own, v_own] + list(far)
    wide = count * 128
    outs = [
        jax.ShapeDtypeStruct((rows, wide), BF),
        jax.ShapeDtypeStruct((2, rows, wide), F32 if far else BF),
    ]
    if far:
        outs.append(jax.ShapeDtypeStruct((2, rows, wide), BF))
    size = 2 * count * rows * rows * (1 if far else 0.5)
    return pl.pallas_call(
        functools.partial(attend_back_kernel, lb if far else 0, kc),
        grid=(count,),
        in_specs=[pl.BlockSpec(memory_space=pltpu.SMEM)]
        + [lse_spec if e is None else spec(e[1] + first) for e in ops],
        out_specs=[spec(0)] + [two] * (len(outs) - 1),
        out_shape=outs,
        scratch_shapes=[pltpu.VMEM((2 if far else 1, 128, rows), BF)]
        + [pltpu.VMEM((rows, 128), F32)] * (4 if far else 2),
        compiler_params=pltpu.CompilerParams(vmem_limit_bytes=40 * 2**20),
        cost_estimate=pl.CostEstimate(
            flops=int(10 * 64 * 5 * size), bytes_accessed=rows * D * 24, transcendentals=int(size)
        ),
        name="attend_back_far" if far else "attend_back_own",
    )(core, *[lse if e is None else e[0] for e in ops])


def place_kernel(count, start_ref, *refs):
    out = refs[count]
    for s in range(count):
        at = start_ref[0] + s
        out[0, jnp.where(at >= count, at - count, at)] = refs[s][0]


def placed(parts, start, dim):
    count = len(parts)
    shape = parts[0].shape
    r, c = shape[-2:]
    g = math.prod(shape[:dim])
    h = math.prod(shape[dim:-2])
    cut = h
    while cut % 2 == 0 and cut * r * c * count > 2**20:
        cut //= 2
    got = pl.pallas_call(
        functools.partial(place_kernel, count),
        grid=(g, h // cut),
        in_specs=[pl.BlockSpec(memory_space=pltpu.SMEM)]
        + [pl.BlockSpec((1, cut, r, c), lambda i, j: (i, j, 0, 0))] * count,
        out_specs=pl.BlockSpec((1, count, cut, r, c), lambda i, j: (i, 0, j, 0, 0)),
        out_shape=jax.ShapeDtypeStruct((g, count, h, r, c), parts[0].dtype),
        compiler_params=pltpu.CompilerParams(vmem_limit_bytes=32 * 2**20),
        cost_estimate=pl.CostEstimate(
            flops=0, bytes_accessed=4 * count * math.prod(shape), transcendentals=0
        ),
        name="place",
    )(start.reshape(1).astype(jnp.int32), *[p.reshape(g, h, r, c) for p in parts])
    return got.reshape(shape[:dim] + (count,) + shape[dim:])


def mlp_kernel(n2_ref, up_ref, down_ref, act_ref, slope_ref, mlp_ref):
    rows = n2_ref.shape[0]

    @pl.when(pl.program_id(0) == 0)
    def _():
        mlp_ref[...] = jnp.zeros_like(mlp_ref)

    for t in range(rows // TQ):
        part = pl.ds(t * TQ, TQ)
        act, slope = gelu_parts(dotf(n2_ref[part, :], up_ref[...], NN))
        act_ref[part, :] = act
        slope_ref[part, :] = slope
        mlp_ref[part, :] += dotf(act, down_ref[...], NN)


def up_spec(wide):
    return pl.BlockSpec((D, wide), lambda i: (0, i))


def down_spec(wide, first=0):
    cuts = D // wide
    return pl.BlockSpec((wide, D), lambda i: (i % cuts, first + i // cuts))


def mlp_forward(n2, w_mlp, wide=768):
    rows = n2.shape[0]
    whole = pl.BlockSpec((rows, D), lambda i: (0, 0))
    across = pl.BlockSpec((rows, wide), lambda i: (0, i))
    return pl.pallas_call(
        mlp_kernel,
        grid=(FF // wide,),
        in_specs=[whole, up_spec(wide), down_spec(wide, FF // D)],
        out_specs=[across, across, whole],
        out_shape=[
            jax.ShapeDtypeStruct((rows, FF), BF),
            jax.ShapeDtypeStruct((rows, FF), BF),
            jax.ShapeDtypeStruct((rows, D), F32),
        ],
        compiler_params=pltpu.CompilerParams(vmem_limit_bytes=40 * 2**20),
        cost_estimate=pl.CostEstimate(
            flops=4 * rows * D * FF,
            bytes_accessed=4 * rows * FF + 4 * D * FF + 6 * rows * D,
            transcendentals=rows * FF,
        ),
        name="mlp_forward",
    )(n2, w_mlp, w_mlp)


def mlp_back_kernel(
    dm_ref, n2_ref, act_ref, slope_ref, up_ref, down_ref, gu_ref, gd_ref, dn_ref, dm_t, n2_t, pre
):
    rows = dm_ref.shape[0]

    @pl.when(pl.program_id(0) == 0)
    def _():
        dm_t[...] = dm_ref[...].astype(F32).T.astype(BF)
        n2_t[...] = n2_ref[...].astype(F32).T.astype(BF)
        dn_ref[...] = jnp.zeros_like(dn_ref)

    for t in range(rows // TQ):
        part = pl.ds(t * TQ, TQ)
        d_act = dotf(dm_ref[part, :], down_ref[...], NT)
        d_pre = (slope_ref[part, :].astype(F32) * d_act).astype(BF)
        pre[part, :] = d_pre
        dn_ref[part, :] += dotf(d_pre, up_ref[...], NT)
    gu_ref[...] = dotf(n2_t[...], pre[...], NN).astype(BF)
    gd_ref[...] = dotf(dm_t[...], act_ref[...], NN).T.astype(BF)


def mlp_backward(d_mlp, n2, act, slope, w_mlp, wide=768):
    rows = n2.shape[0]
    whole = pl.BlockSpec((rows, D), lambda i: (0, 0))
    across = pl.BlockSpec((rows, wide), lambda i: (0, i))
    return pl.pallas_call(
        mlp_back_kernel,
        grid=(FF // wide,),
        in_specs=[whole, whole, across, across, up_spec(wide), down_spec(wide, FF // D)],
        out_specs=[up_spec(wide), down_spec(wide), whole],
        out_shape=[
            jax.ShapeDtypeStruct((D, FF), BF),
            jax.ShapeDtypeStruct((D, FF), BF),
            jax.ShapeDtypeStruct((rows, D), F32),
        ],
        scratch_shapes=[
            pltpu.VMEM((D, rows), BF),
            pltpu.VMEM((D, rows), BF),
            pltpu.VMEM((rows, wide), BF),
        ],
        compiler_params=pltpu.CompilerParams(vmem_limit_bytes=48 * 2**20),
        cost_estimate=pl.CostEstimate(
            flops=8 * rows * D * FF,
            bytes_accessed=4 * rows * FF + 8 * D * FF + 8 * rows * D,
            transcendentals=0,
        ),
        name="mlp_backward",
    )(d_mlp, n2, act, slope, w_mlp, w_mlp)


def norm_parts(rows):
    scale = lax.rsqrt(jnp.mean(rows * rows, axis=-1, keepdims=True) + EPS)
    return rows * scale, scale


def norm_back(d_out, unit, scale, gain):
    d_gain = jnp.sum(d_out * unit, axis=0)
    d_unit = d_out * gain
    d_rows = scale * (d_unit - unit * jnp.mean(d_unit * unit, axis=-1, keepdims=True))
    return d_rows, d_gain


def gelu_parts(pre):
    c = math.sqrt(2.0 / math.pi)
    sq = pre * pre
    t = jnp.tanh(c * pre * (1.0 + 0.044715 * sq))
    act = 0.5 * pre * (1.0 + t)
    slope = 0.5 * (1.0 + t) + 0.5 * pre * (1.0 - t * t) * (c * (1.0 + 3 * 0.044715 * sq))
    return act.astype(BF), slope.astype(BF)


def after(value, *others):
    return lax.optimization_barrier((value, *others))[0]


def forward_first(rows, gain_a, w_a):
    unit_a, _ = norm_parts(rows)
    n1 = (unit_a * gain_a).astype(BF)
    return n1, dotf(n1, w_a[:, D : 3 * D], NN).astype(BF)


def forward_second(rows, gain_b, w_a, o):
    branch = dotf(o, w_a[:, 3 * D : 4 * D], NN)
    mid = rows + branch
    unit_b, _ = norm_parts(mid)
    return branch, mid, (unit_b * gain_b).astype(BF)


def back_mlp(mid, weights, gain_b, saved, mlp_low, d_top, d_extra):
    o, n2, act, slope = saved
    w_a, w_mlp = weights
    g_up, g_down, d_n2 = mlp_backward(mlp_low, n2, act, slope, w_mlp)
    unit_b, scale_b = norm_parts(mid)
    d_mid, g_b = norm_back(d_n2, unit_b, scale_b, gain_b)
    if d_top is not None:
        d_mid = d_mid + d_top
    d_branch = (d_mid if d_extra is None else d_mid + d_extra).astype(BF)
    do = dotf(d_branch, w_a[:, 3 * D : 4 * D], NT).astype(BF)
    g_out = dotf(o, d_branch, TN).astype(BF)
    return d_mid, do, g_out, g_up, g_down, g_b


def back_qkv(rows, w_a, gain_a, n1, d_q, d_kv, d_mid):
    g_q = dotf(n1, d_q, TN).astype(BF)
    g_kv = dotf(n1, d_kv, TN).astype(BF)
    unit_a, scale_a = norm_parts(rows)
    d_n1 = dotf(d_q, w_a[:, :D], NT) + dotf(d_kv, w_a[:, D : 3 * D], NT)
    d_rows, g_a = norm_back(d_n1, unit_a, scale_a, gain_a)
    return d_rows + d_mid, g_q, g_kv, g_a


def ahead(value, axis, size, step):
    return lax.ppermute(value, axis, [(i, (i - step) % size) for i in range(size)])


def solution(mesh):
    dp, seq = mesh.shape["dp"], mesh.shape["seq"]
    y_n = dp // 2
    x_n = y_n if seq % y_n == 0 else 1
    z_n = seq // x_n
    half = seq // 2
    ways = dp * seq
    inner = Mesh(mesh.devices.reshape(y_n, 2, z_n, x_n), ("y", "core", "z", "x"))
    every = ("y", "core", "z", "x")
    home_axes = ("core", "z", "x")
    lb = LEN // seq

    def route(t):
        pairs = []
        for c in range(2):
            for s in range(seq):
                block = s // 2
                core = (s ^ block) & 1
                pairs.append((c * seq + s, core * seq + 2 * ((block + t) % half) + c))
        return pairs

    routes = [route(t) for t in range(half)]

    def swap_core(value):
        return lax.ppermute(value, "core", [(0, 1), (1, 0)])

    def all_sum(value):
        for axis, size in (("core", 2), ("x", x_n), ("y", y_n), ("z", z_n)):
            value = sum(
                (ahead(value, axis, size, s) for s in range(1, size)), start=value
            )
        return value

    def body(
        tokens, cotangent, picked_ids, lengths,
        qkv_w, out_w, up_w, down_w, vectors,
        qkv_mom, out_mom, up_mom, down_mom, vec_mom,
        qkv_avg, out_avg, up_avg, down_avg, vec_avg,
    ):
        y, core, z, x = (lax.axis_index(a) for a in every)
        chip = z * x_n + x
        seq_id = chip // 2
        group = chip % 2
        core_arr = jnp.full((1,), core, jnp.int32)
        piece = D // ways

        def grown(value, axis, size, place, dim):
            if size == 1:
                return jnp.expand_dims(value, dim)
            return placed(
                [value] + [ahead(value, axis, size, s) for s in range(1, size)], place, dim
            )

        def spread_z(shard):
            return grown(shard, "z", z_n, z, 0)

        def spread_x(value, x_first):
            return grown(value, "x", x_n, x, 1 if x_first else 2)

        def spread_y(value):
            return grown(value, "y", y_n, y, 0)

        def spread_core(value):
            value = grown(value, "core", 2, core, 1)
            return value.reshape(ways * value.shape[-2], value.shape[-1])

        def shard_a(layer):
            return jnp.concatenate(
                [qkv_w[layer].transpose(1, 0, 2).reshape(piece, 3 * D), out_w[layer]], axis=1
            ).astype(BF)

        def shard_mlp(layer):
            up = up_w[layer].astype(BF).reshape(piece, ways, 4, piece).swapaxes(1, 2)
            down = down_w[layer].astype(BF).reshape(4, piece, D).swapaxes(0, 1)
            return jnp.concatenate([up.reshape(piece, FF), down.reshape(piece, FF)], axis=1)

        def gather_mlp(shard):
            return lax.all_gather(shard, every, axis=0, tiled=True)

        def come(source):
            by_seq = source.transpose(1, 0, 2)
            got = []
            for t in range(half):
                sent = lax.dynamic_index_in_dim(by_seq, (chip // 2 + t) % half, 0, keepdims=False)
                got.append(lax.ppermute(sent, home_axes, routes[t]))
            return got

        def own_rows(got):
            return placed(got[:1] + got[:0:-1], seq_id, 0).reshape(half * lb, D)

        def leave(rows):
            got = []
            for t in range(half):
                sent = lax.dynamic_slice(rows, (((seq_id - t) % half) * lb, 0), (lb, D))
                got.append(lax.ppermute(sent, home_axes, [(b, a) for a, b in routes[t]]))
            return got

        def arrived(got):
            return placed(got, chip // 2, 0).transpose(1, 0, 2)

        gains_row = jnp.pad(vectors.T, ((0, 0), (0, 128 - 5))).astype(BF)
        mlp0 = gather_mlp(shard_mlp(0))
        chips_a = spread_z(jnp.concatenate([shard_a(0), gains_row], axis=1))
        chips_a = spread_x(chips_a, True)
        own_x = own_rows(come(tokens))
        next_a = after(shard_a(1), own_x)
        chips_b = spread_z(next_a)
        chips_a = after(spread_y(chips_a), own_x, chips_b)
        full_a = spread_core(chips_a)
        gains = full_a[:, 4 * D : 4 * D + 5].T.astype(F32)
        meta = jnp.concatenate([picked_ids, lengths[:, None]], axis=1)
        meta = lax.dynamic_index_in_dim(
            jnp.where(group == core, meta, swap_core(meta)), seq_id, 0, keepdims=False
        )
        picks, length = meta[:-1], meta[-1]
        row_ids = jnp.arange(half * lb, dtype=jnp.int32)
        block = row_ids // lb
        places = (2 * block + ((core + block) & 1)) * lb + row_ids % lb
        chosen = (picks[:, None] == places[None, :]).astype(BF)
        live = (places < length).astype(F32)[:, None]

        def at_picks(rows):
            part = dotf(chosen, rows, NN).astype(BF)
            return part + swap_core(part)

        def to_rows(values):
            return dotf(chosen, values, TN)

        mlp1 = gather_mlp(after(shard_mlp(1), full_a))
        x_low = at_picks(own_x)
        x_rows = x_low.astype(F32)
        gate = jax.nn.sigmoid(jnp.sum(x_rows * gains[2], axis=-1, keepdims=True))
        n1_0, kv0 = forward_first(x_rows, gains[0], full_a)
        q0 = dotf(n1_0, full_a[:, :D], NN).astype(BF)
        chips_b = spread_y(after(chips_b, x_low))
        own0 = ((q0, 0), (kv0, 0), (kv0, 6))
        o0, lse0 = attend(*own0, (), core_arr, lb)
        branch0, mid0, n2_0 = forward_second(x_rows, gains[1], full_a, o0)
        chips_b = spread_x(after(chips_b, q0), False)
        act0, slope0, out0 = mlp_forward(n2_0, mlp0)
        both0 = branch0 + out0
        delta = (gate * both0).astype(BF)
        mixed = own_x.astype(F32) + to_rows(delta)

        full_b = spread_core(after(chips_b, n2_0))
        cot_sent = come(after(cotangent, full_b))
        n1_1, kv1 = forward_first(mixed, gains[3], full_b)
        far = swap_core(kv1)
        far1 = ((far, 0), (far, 6))
        q1 = dotf(n1_1, full_b[:, :D], NN).astype(BF)
        own1 = ((q1, 0), (kv1, 0), (kv1, 6))
        o1, lse1 = attend(*own1, far1, core_arr, lb)
        branch1, mid1, n2_1 = forward_second(mixed, gains[4], full_b, o1)
        act1, slope1, out1 = mlp_forward(n2_1, mlp1)
        act_sent = leave((live * (mid1 + out1)).astype(BF))
        d_top = live * own_rows([after(c, o1) for c in cot_sent]).astype(F32)

        def by_shard(grad):
            return grad.reshape(y_n, 2, z_n, x_n, grad.shape[0] // ways, grad.shape[1])

        def at(grads, which, dim):
            return jnp.concatenate(
                [lax.dynamic_index_in_dim(g, which, dim, keepdims=False) for g in grads], axis=-1
            )

        def over_core(*grads):
            grads = [by_shard(g) for g in grads]
            got = swap_core(at(grads, 1 - core, 1))
            return (at(grads, core, 1).astype(F32) + got.astype(F32)).astype(BF)

        def of_core(*grads):
            return at([by_shard(g) for g in grads], core, 1)

        def over(value, axis, size, place, dim, kind=BF, late=()):
            total = at([value], place, dim).astype(F32)
            for s in range(1, size):
                sent = at([value], (place + size - s) % size, dim)
                total = total + after(ahead(sent, axis, size, s), *late).astype(F32)
            return total.astype(kind)

        def first_way(value, x_first):
            return over(value, "x", x_n, x, 2) if x_first else over(value, "y", y_n, y, 0)

        def second_way(value, x_first):
            return over(value, "y", y_n, y, 0) if x_first else over(value, "x", x_n, x, 1)

        def last_way(value, *late):
            return over(value, "z", z_n, z, 0, F32, late)

        def along(value, x_first):
            return last_way(second_way(first_way(value, x_first), x_first))

        def columns(*vectors):
            return jnp.pad(jnp.stack(vectors, 1), ((0, 0), (0, 128 - len(vectors)))).astype(BF)

        d_mid1, do1, g_out1, g_up1, g_down1, g_b1 = back_mlp(
            mid1, (full_b, mlp1), gains[4], (o1, n2_1, act1, slope1), d_top.astype(BF), d_top, None
        )
        up1, down1 = over_core(g_up1), over_core(g_down1)
        do1 = after(do1, up1, down1)
        up1, down1 = first_way(up1, False), first_way(down1, True)
        parts = []
        for first, count in ((0, 4), (4, 2)):
            dq, d_own, d_far = attend_back(
                own1[0], (do1, 0), (o1, 0), lse1, own1[1], own1[2], far1, core_arr, lb, first, count
            )
            parts.append((dq, d_own, swap_core(d_far)))
            up1, down1 = after(up1, dq), after(down1, dq)
            if first == 0:
                act_sent = [after(a, dq) for a in act_sent]
                do1 = after(do1, up1, down1, dq, *act_sent)
                up1, down1 = second_way(up1, False), second_way(down1, True)
        d_q1 = jnp.concatenate([parts[0][0], dq], axis=1)
        sums = [(d_own + back.astype(F32)).astype(BF) for _, d_own, back in parts]
        d_kv1 = jnp.concatenate([s[0] for s in sums] + [s[1] for s in sums], axis=1)
        d_mixed, g_q1, g_kv1, g_a1 = back_qkv(mixed, full_b, gains[3], n1_1, d_q1, d_kv1, d_mid1)
        head1 = over_core(g_q1, g_kv1, g_out1, columns(g_a1, g_b1))

        d_delta = at_picks(d_mixed.astype(BF)).astype(F32)
        gated = gate * d_delta
        d_logit = gate * (1.0 - gate) * jnp.sum(d_delta * both0, axis=-1, keepdims=True)
        activations = arrived([after(a, d_mixed) for a in act_sent])
        pair1 = jnp.concatenate([up1, down1], axis=-1)
        head1a = first_way(head1[..., : 2 * D], False)
        head1b = first_way(head1[..., 2 * D :], True)
        d_mid0, do0, g_out0, g_up0, g_down0, g_b0 = back_mlp(
            mid0, (full_a, mlp0), gains[1], (o0, n2_0, act0, slope0), gated.astype(BF), None, gated
        )
        up0, down0 = first_way(of_core(g_up0), False), first_way(of_core(g_down0), True)
        dq, d_kv = attend_back(
            own0[0], (do0, 0), (o0, 0), lse0, own0[1], own0[2], (), core_arr, lb, 0, PAIRS
        )
        head1a, head1b = second_way(after(head1a, dq), False), second_way(after(head1b, dq), True)
        d_kv0 = jnp.concatenate([d_kv[0], d_kv[1]], axis=1)
        d_rows0, g_q0, g_kv0, g_a0 = back_qkv(x_rows, full_a, gains[0], n1_0, dq, d_kv0, d_mid0)
        g_r = jnp.sum(d_logit * x_rows, axis=0)
        d_chosen = (d_rows0 + d_logit * gains[2]).astype(BF)
        grad_rows = (d_mixed + to_rows(d_chosen)).astype(BF)
        pair1 = last_way(pair1, grad_rows)
        grad_sent = leave(grad_rows)
        up0, down0 = second_way(up0, False), second_way(down0, True)
        head0a = after(of_core(g_q0, g_kv0[:, :D]), grad_rows, up0, down0)
        head0b = of_core(g_kv0[:, D:], g_out0, columns(g_a0, g_b0, g_r))
        head0b = after(head0b, grad_rows, up0, down0)
        early = jnp.concatenate([up0, down0, head1a, head1b], axis=-1)
        head0a, head0b = first_way(head0a, False), first_way(head0b, True)
        early = last_way(after(early, *grad_sent), head0a, head0b)
        head0a, head0b = second_way(head0a, False), second_way(head0b, True)
        head0 = last_way(after(jnp.concatenate([head0a, head0b], axis=-1), early))
        squares = sum(jnp.sum(v * v) for v in (early, head0, pair1))
        up0, down0, head1 = early[:, :FF], early[:, FF : 2 * FF], early[:, 2 * FF :]
        up1, down1 = pair1[:, :FF], pair1[:, FF:]
        input_grad = arrived(grad_sent).astype(F32)

        def unmixed(up):
            return up.reshape(piece, 4, ways, piece).swapaxes(1, 2).reshape(piece, FF)

        def unpacked(down):
            return down.reshape(piece, 4, D).swapaxes(0, 1).reshape(4 * piece, D)

        shards = [
            jnp.stack([h[:, : 3 * D].reshape(piece, 3, D).transpose(1, 0, 2) for h in (head0, head1)]),
            jnp.stack([head0[:, 3 * D : 4 * D], head1[:, 3 * D : 4 * D]]),
            jnp.stack([unmixed(up0), unmixed(up1)]),
            jnp.stack([unpacked(down0), unpacked(down1)]),
            jnp.concatenate([head0[:, 4 * D : 4 * D + 3].T, head1[:, 4 * D : 4 * D + 2].T]),
        ]
        grad_norm = jnp.sqrt(all_sum(squares.reshape(1, 1))[0, 0])
        factor = 1.0 / jnp.maximum(grad_norm, 1.0)
        base_rate = math.sqrt(NPARAMS / D)
        rates = (base_rate, math.sqrt(NPARAMS * LEN / (8 * D)), base_rate, base_rate, base_rate)
        masters = (qkv_w, out_w, up_w, down_w, vectors)
        moms = (qkv_mom, out_mom, up_mom, down_mom, vec_mom)
        avgs = (qkv_avg, out_avg, up_avg, down_avg, vec_avg)
        new_w, new_m, new_z = [], [], []
        for weight, grad, mom, avg, rate in zip(masters, shards, moms, avgs, rates):
            clipped = grad * factor
            m = 0.5 * mom + clipped
            w = weight - rate * (clipped + 0.5 * m)
            new_w.append(w)
            new_m.append(m)
            new_z.append(0.5 * avg + 0.5 * w)
        return (activations, input_grad, grad_norm, *new_w, *new_m, *new_z)

    group_spec = ("y", "core")
    pos_spec = ("z", "x")
    rows_spec = P(pos_spec, group_spec, None)
    param_specs = (
        P(None, None, every, None),
        P(None, every, None),
        P(None, every, None),
        P(None, every, None),
        P(None, every),
    )
    return jax.shard_map(
        body,
        mesh=inner,
        in_specs=(rows_spec, rows_spec, P(group_spec, None), P(group_spec)) + param_specs * 3,
        out_specs=(rows_spec, rows_spec, P()) + param_specs * 3,
        check_vma=False,
    )
```

```python
import functools
import math

import jax
import jax.numpy as jnp
from jax import lax
from jax.experimental import pallas as pl
from jax.experimental.pallas import tpu as pltpu
from jax.sharding import Mesh
from jax.sharding import PartitionSpec as P

D = 768
FF = 3072
LEN = 2048
NPARAMS = 14159616
EPS = 1e-06
PAIRS = 6
TQ = 256
NN = (((1,), (0,)), ((), ()))
NT = (((1,), (1,)), ((), ()))
TN = (((0,), (0,)), ((), ()))
BF = jnp.bfloat16
F32 = jnp.float32


def dotf(left, right, dims):
    return lax.dot_general(left, right, dims, preferred_element_type=F32)


def far_mask(core, tile, lb, q_axis):
    shift = lb.bit_length() - 1
    iq = lax.broadcasted_iota(jnp.int32, (TQ, TQ), q_axis) >> shift
    ik = lax.broadcasted_iota(jnp.int32, (TQ, TQ), 1 - q_axis) >> shift
    odd = (core + tile * (TQ >> shift) + iq) & 1
    return (iq > ik) | ((iq == ik) & (odd == 1))


def attend_kernel(lb, core_ref, *refs):
    if lb:
        q_ref, ko, vo, kf, vf, o_ref, lse_ref = refs
    else:
        q_ref, ko, vo, o_ref, lse_ref = refs
    rows = q_ref.shape[0]
    lane = lax.broadcasted_iota(jnp.int32, (TQ, 128), 1)
    tri = lax.broadcasted_iota(jnp.int32, (TQ, TQ), 0) >= lax.broadcasted_iota(
        jnp.int32, (TQ, TQ), 1
    )
    for t in range(rows // TQ):
        n = t * TQ
        q = q_ref[pl.ds(n, TQ), :] * BF(0.125)
        outs = []
        cols = []
        if lb:
            fm = far_mask(core_ref[0], t, lb, 0)
        for h in range(2):
            qm = jnp.where((lane >= 64) if h else (lane < 64), q, BF(0))
            segs = []
            if t:
                segs.append((dotf(qm, ko[pl.ds(0, n), :], NT), vo[pl.ds(0, n), :]))
            segs.append(
                (jnp.where(tri, dotf(qm, ko[pl.ds(n, TQ), :], NT), -1e30), vo[pl.ds(n, TQ), :])
            )
            if lb:
                if t:
                    segs.append((dotf(qm, kf[pl.ds(0, n), :], NT), vf[pl.ds(0, n), :]))
                segs.append(
                    (jnp.where(fm, dotf(qm, kf[pl.ds(n, TQ), :], NT), -1e30), vf[pl.ds(n, TQ), :])
                )
            top = functools.reduce(
                jnp.maximum, [jnp.max(s, axis=1, keepdims=True) for s, _ in segs]
            )
            total = 0.0
            acc = 0.0
            for s, v in segs:
                e = jnp.exp(s - top)
                total = total + jnp.sum(e, axis=1, keepdims=True)
                acc = acc + dotf(e.astype(BF), v, NN)
            outs.append(acc * (1.0 / total))
            cols.append(jnp.broadcast_to(top + jnp.log(total), (TQ, 128)))
        o_ref[pl.ds(n, TQ), :] = jnp.where(lane < 64, outs[0], outs[1]).astype(BF)
        for h in range(2):
            lse_ref[0, pl.ds(h, 1), pl.ds(n, TQ)] = cols[h].T[0:1, :]


def attend(q, k_own, v_own, far, core, lb):
    rows = q[0].shape[0]
    ops = [q, k_own, v_own] + list(far)

    def spec(off):
        return pl.BlockSpec((rows, 128), lambda i, off=off: (0, off + i))

    size = 12 * rows * rows * (1 if far else 0.5)
    return pl.pallas_call(
        functools.partial(attend_kernel, lb if far else 0),
        grid=(PAIRS,),
        in_specs=[pl.BlockSpec(memory_space=pltpu.SMEM)] + [spec(o) for _, o in ops],
        out_specs=[spec(0), pl.BlockSpec((1, 2, rows), lambda i: (i, 0, 0))],
        out_shape=[
            jax.ShapeDtypeStruct((rows, D), BF),
            jax.ShapeDtypeStruct((PAIRS, 2, rows), F32),
        ],
        compiler_params=pltpu.CompilerParams(vmem_limit_bytes=40 * 2**20),
        cost_estimate=pl.CostEstimate(
            flops=int(4 * 64 * 6 * size), bytes_accessed=rows * D * 12, transcendentals=int(size)
        ),
        name="attend_far" if far else "attend_own",
    )(core, *[a for a, _ in ops])


def attend_back_kernel(lb, kc, core_ref, *refs):
    if lb:
        q_ref, do_ref, o_ref, lse_ref, ko, vo, kf, vf = refs[:8]
        dq_ref, d_own, d_far, k_t, aok, aov, afk, afv = refs[8:]
        parts = [(ko, vo, aok, aov, 0), (kf, vf, afk, afv, 1)]
    else:
        q_ref, do_ref, o_ref, lse_ref, ko, vo, dq_ref, d_own, k_t, aok, aov = refs
        parts = [(ko, vo, aok, aov, 0)]
    rows = q_ref.shape[0]
    lane = lax.broadcasted_iota(jnp.int32, (TQ, 128), 1)
    tri = lax.broadcasted_iota(jnp.int32, (TQ, TQ), 1) >= lax.broadcasted_iota(
        jnp.int32, (TQ, TQ), 0
    )
    for k, _, ak, av, s in parts:
        k_t[s] = k[...].astype(F32).T.astype(BF)
        ak[...] = jnp.zeros_like(ak)
        av[...] = jnp.zeros_like(av)
    for t in range(rows // TQ):
        n = t * TQ
        q = q_ref[pl.ds(n, TQ), :] * BF(0.125)
        do = do_ref[pl.ds(n, TQ), :]
        prod = (do.astype(F32) * o_ref[pl.ds(n, TQ), :].astype(F32)).T
        dqs = []
        if lb:
            fm = far_mask(core_ref[0], t, lb, 1)
        for h in range(2):
            half = (lane >= 64) if h else (lane < 64)
            qm = jnp.where(half, q, BF(0))
            dom = jnp.where(half, do, BF(0))
            inner = jnp.sum(prod[64 * h : 64 * h + 64], axis=0, keepdims=True)
            lse = lse_ref[0, pl.ds(h, 1), pl.ds(n, TQ)]
            dq_t = 0.0
            for k, v, ak, av, s in parts:
                spans = []
                a = 0
                while a < n:
                    w = min(kc, n - a)
                    spans.append((a, w, None))
                    a += w
                spans.append((n, TQ, fm if s else tri))
                for a, w, mask in spans:
                    p = jnp.exp(dotf(k[pl.ds(a, w), :], qm, NT) - lse)
                    if mask is not None:
                        p = jnp.where(mask, p, 0.0)
                    dp = dotf(v[pl.ds(a, w), :], dom, NT)
                    ds = (p * (dp - inner)).astype(BF)
                    av[pl.ds(a, w), :] += dotf(p.astype(BF), dom, NN)
                    ak[pl.ds(a, w), :] += dotf(ds, qm, NN)
                    dq_t = dq_t + dotf(k_t[s, 64 * h : 64 * h + 64, a : a + w], ds, NN)
            dqs.append(dq_t)
        dq_ref[pl.ds(n, TQ), :] = (jnp.concatenate(dqs, axis=0) * 0.125).T.astype(BF)
    d_own[0] = aok[...].astype(d_own.dtype)
    d_own[1] = aov[...].astype(d_own.dtype)
    if lb:
        d_far[0] = afk[...].astype(BF)
        d_far[1] = afv[...].astype(BF)


def attend_back(q, do, o, lse, k_own, v_own, far, core, lb, first, count, kc=512):
    rows = do[0].shape[0]

    def spec(off):
        return pl.BlockSpec((rows, 128), lambda i, off=off: (0, off + i))

    two = pl.BlockSpec((2, rows, 128), lambda i: (0, 0, i))
    lse_spec = pl.BlockSpec((1, 2, rows), lambda i: (i + first, 0, 0))
    ops = [q, do, o, None, k_own, v_own] + list(far)
    wide = count * 128
    outs = [
        jax.ShapeDtypeStruct((rows, wide), BF),
        jax.ShapeDtypeStruct((2, rows, wide), F32 if far else BF),
    ]
    if far:
        outs.append(jax.ShapeDtypeStruct((2, rows, wide), BF))
    size = 2 * count * rows * rows * (1 if far else 0.5)
    return pl.pallas_call(
        functools.partial(attend_back_kernel, lb if far else 0, kc),
        grid=(count,),
        in_specs=[pl.BlockSpec(memory_space=pltpu.SMEM)]
        + [lse_spec if e is None else spec(e[1] + first) for e in ops],
        out_specs=[spec(0)] + [two] * (len(outs) - 1),
        out_shape=outs,
        scratch_shapes=[pltpu.VMEM((2 if far else 1, 128, rows), BF)]
        + [pltpu.VMEM((rows, 128), F32)] * (4 if far else 2),
        compiler_params=pltpu.CompilerParams(vmem_limit_bytes=40 * 2**20),
        cost_estimate=pl.CostEstimate(
            flops=int(10 * 64 * 5 * size), bytes_accessed=rows * D * 24, transcendentals=int(size)
        ),
        name="attend_back_far" if far else "attend_back_own",
    )(core, *[lse if e is None else e[0] for e in ops])


def place_kernel(count, start_ref, *refs):
    out = refs[count]
    for s in range(count):
        at = start_ref[0] + s
        out[0, jnp.where(at >= count, at - count, at)] = refs[s][0]


def placed(parts, start, dim):
    count = len(parts)
    shape = parts[0].shape
    r, c = shape[-2:]
    g = math.prod(shape[:dim])
    h = math.prod(shape[dim:-2])
    cut = h
    while cut % 2 == 0 and cut * r * c * count > 2**20:
        cut //= 2
    got = pl.pallas_call(
        functools.partial(place_kernel, count),
        grid=(g, h // cut),
        in_specs=[pl.BlockSpec(memory_space=pltpu.SMEM)]
        + [pl.BlockSpec((1, cut, r, c), lambda i, j: (i, j, 0, 0))] * count,
        out_specs=pl.BlockSpec((1, count, cut, r, c), lambda i, j: (i, 0, j, 0, 0)),
        out_shape=jax.ShapeDtypeStruct((g, count, h, r, c), parts[0].dtype),
        compiler_params=pltpu.CompilerParams(vmem_limit_bytes=32 * 2**20),
        cost_estimate=pl.CostEstimate(
            flops=0, bytes_accessed=4 * count * math.prod(shape), transcendentals=0
        ),
        name="place",
    )(start.reshape(1).astype(jnp.int32), *[p.reshape(g, h, r, c) for p in parts])
    return got.reshape(shape[:dim] + (count,) + shape[dim:])


def mlp_kernel(n2_ref, up_ref, down_ref, act_ref, slope_ref, mlp_ref):
    rows = n2_ref.shape[0]

    @pl.when(pl.program_id(0) == 0)
    def _():
        mlp_ref[...] = jnp.zeros_like(mlp_ref)

    for t in range(rows // TQ):
        part = pl.ds(t * TQ, TQ)
        act, slope = gelu_parts(dotf(n2_ref[part, :], up_ref[...], NN))
        act_ref[part, :] = act
        slope_ref[part, :] = slope
        mlp_ref[part, :] += dotf(act, down_ref[...], NN)


def up_spec(wide):
    return pl.BlockSpec((D, wide), lambda i: (0, i))


def down_spec(wide, first=0):
    cuts = D // wide
    return pl.BlockSpec((wide, D), lambda i: (i % cuts, first + i // cuts))


def mlp_forward(n2, w_mlp, wide=768):
    rows = n2.shape[0]
    whole = pl.BlockSpec((rows, D), lambda i: (0, 0))
    across = pl.BlockSpec((rows, wide), lambda i: (0, i))
    return pl.pallas_call(
        mlp_kernel,
        grid=(FF // wide,),
        in_specs=[whole, up_spec(wide), down_spec(wide, w_mlp[2])],
        out_specs=[across, across, whole],
        out_shape=[
            jax.ShapeDtypeStruct((rows, FF), BF),
            jax.ShapeDtypeStruct((rows, FF), BF),
            jax.ShapeDtypeStruct((rows, D), F32),
        ],
        compiler_params=pltpu.CompilerParams(vmem_limit_bytes=56 * 2**20),
        cost_estimate=pl.CostEstimate(
            flops=4 * rows * D * FF,
            bytes_accessed=4 * rows * FF + 4 * D * FF + 6 * rows * D,
            transcendentals=rows * FF,
        ),
        name="mlp_forward",
    )(n2, w_mlp[0], w_mlp[1])


def mlp_back_kernel(
    dm_ref, n2_ref, act_ref, slope_ref, up_ref, down_ref, gu_ref, gd_ref, dn_ref, dm_t, n2_t, pre
):
    rows = dm_ref.shape[0]

    @pl.when(pl.program_id(0) == 0)
    def _():
        dm_t[...] = dm_ref[...].astype(F32).T.astype(BF)
        n2_t[...] = n2_ref[...].astype(F32).T.astype(BF)
        dn_ref[...] = jnp.zeros_like(dn_ref)

    for t in range(rows // TQ):
        part = pl.ds(t * TQ, TQ)
        d_act = dotf(dm_ref[part, :], down_ref[...], NT)
        d_pre = (slope_ref[part, :].astype(F32) * d_act).astype(BF)
        pre[part, :] = d_pre
        dn_ref[part, :] += dotf(d_pre, up_ref[...], NT)
    gu_ref[...] = dotf(n2_t[...], pre[...], NN).astype(BF)
    gd_ref[...] = dotf(dm_t[...], act_ref[...], NN).T.astype(BF)


def mlp_backward(d_mlp, n2, act, slope, w_mlp, wide=768):
    rows = n2.shape[0]
    whole = pl.BlockSpec((rows, D), lambda i: (0, 0))
    across = pl.BlockSpec((rows, wide), lambda i: (0, i))
    return pl.pallas_call(
        mlp_back_kernel,
        grid=(FF // wide,),
        in_specs=[whole, whole, across, across, up_spec(wide), down_spec(wide, w_mlp[2])],
        out_specs=[up_spec(wide), down_spec(wide), whole],
        out_shape=[
            jax.ShapeDtypeStruct((D, FF), BF),
            jax.ShapeDtypeStruct((D, FF), BF),
            jax.ShapeDtypeStruct((rows, D), F32),
        ],
        scratch_shapes=[
            pltpu.VMEM((D, rows), BF),
            pltpu.VMEM((D, rows), BF),
            pltpu.VMEM((rows, wide), BF),
        ],
        compiler_params=pltpu.CompilerParams(vmem_limit_bytes=56 * 2**20),
        cost_estimate=pl.CostEstimate(
            flops=8 * rows * D * FF,
            bytes_accessed=4 * rows * FF + 8 * D * FF + 8 * rows * D,
            transcendentals=0,
        ),
        name="mlp_backward",
    )(d_mlp, n2, act, slope, w_mlp[0], w_mlp[1])


def norm_parts(rows):
    scale = lax.rsqrt(jnp.mean(rows * rows, axis=-1, keepdims=True) + EPS)
    return rows * scale, scale


def norm_back(d_out, unit, scale, gain):
    d_gain = jnp.sum(d_out * unit, axis=0)
    d_unit = d_out * gain
    d_rows = scale * (d_unit - unit * jnp.mean(d_unit * unit, axis=-1, keepdims=True))
    return d_rows, d_gain


def gelu_parts(pre):
    c = math.sqrt(2.0 / math.pi)
    k = 0.044715 * c
    sq = pre * pre
    h = 0.5 * jnp.tanh(pre * (c + k * sq)) + 0.5
    act = pre * h
    slope = h + (act * (1.0 - h)) * (2.0 * c + (6.0 * k) * sq)
    return act.astype(BF), slope.astype(BF)


def after(value, *others):
    return lax.optimization_barrier((value, *others))[0]


def forward_first(rows, gain_a, w_a):
    unit_a, _ = norm_parts(rows)
    n1 = (unit_a * gain_a).astype(BF)
    return n1, dotf(n1, w_a[:, D : 3 * D], NN).astype(BF)


def forward_second(rows, gain_b, w_a, o):
    branch = dotf(o, w_a[:, 3 * D : 4 * D], NN)
    mid = rows + branch
    unit_b, _ = norm_parts(mid)
    return branch, mid, (unit_b * gain_b).astype(BF)


def back_mlp(mid, weights, gain_b, saved, mlp_low, d_top, d_extra):
    o, n2, act, slope = saved
    w_a, w_mlp = weights
    g_up, g_down, d_n2 = mlp_backward(mlp_low, n2, act, slope, w_mlp)
    unit_b, scale_b = norm_parts(mid)
    d_mid, g_b = norm_back(d_n2, unit_b, scale_b, gain_b)
    if d_top is not None:
        d_mid = d_mid + d_top
    d_branch = (d_mid if d_extra is None else d_mid + d_extra).astype(BF)
    do = dotf(d_branch, w_a[:, 3 * D : 4 * D], NT).astype(BF)
    g_out = dotf(o, d_branch, TN).astype(BF)
    return d_mid, do, g_out, g_up, g_down, g_b


def back_qkv(rows, w_a, gain_a, n1, d_q, d_kv, d_mid):
    g_q = dotf(n1, d_q, TN).astype(BF)
    g_kv = dotf(n1, d_kv, TN).astype(BF)
    unit_a, scale_a = norm_parts(rows)
    d_n1 = dotf(d_q, w_a[:, :D], NT) + dotf(d_kv, w_a[:, D : 3 * D], NT)
    d_rows, g_a = norm_back(d_n1, unit_a, scale_a, gain_a)
    return d_rows + d_mid, g_q, g_kv, g_a


def ahead(value, axis, size, step):
    return lax.ppermute(value, axis, [(i, (i - step) % size) for i in range(size)])


def solution(mesh):
    dp, seq = mesh.shape["dp"], mesh.shape["seq"]
    y_n = dp // 2
    x_n = y_n if seq % y_n == 0 else 1
    z_n = seq // x_n
    half = seq // 2
    ways = dp * seq
    inner = Mesh(
        mesh.devices.reshape(y_n, 2, z_n, x_n // 2, 2), ("y", "core", "z", "xh", "xl")
    )
    both_x = ("xh", "xl")
    every = ("y", "core", "z", "xh", "xl")
    lb = LEN // seq

    def route(t):
        pairs = []
        for c in range(2):
            for s in range(seq):
                block = s // 2
                pairs.append((c * seq + s, ((s ^ block) & 1) * seq + 2 * ((block + t) % half) + c))
        return pairs

    routes = [route(t) for t in range(half)]

    def turn(odd):
        return [(c * 2 + e, (e ^ odd) * 2 + c) for c in range(2) for e in range(2)]

    def swap_core(value):
        return lax.ppermute(value, "core", [(0, 1), (1, 0)])

    def all_sum(value):
        pair = [
            lax.ppermute(
                value,
                ("core", *both_x),
                [
                    (c * x_n + i, ((c + dc) % 2) * x_n + (i + dx) % x_n)
                    for c in range(2)
                    for i in range(x_n)
                ],
            )
            for dc in range(2)
            for dx in range(x_n)
            if dc or dx
        ]
        value = sum(pair, start=value)
        for axis, size in (("y", y_n), ("z", z_n)):
            value = sum(
                (ahead(value, axis, size, s) for s in range(1, size)), start=value
            )
        return value

    def body(
        tokens, cotangent, picked_ids, lengths,
        qkv_w, out_w, up_w, down_w, vectors,
        qkv_mom, out_mom, up_mom, down_mom, vec_mom,
        qkv_avg, out_avg, up_avg, down_avg, vec_avg,
    ):
        y, core, z, x = (lax.axis_index(a) for a in ("y", "core", "z", both_x))
        chip = z * x_n + x
        seq_id = chip // 2
        group = chip % 2
        core_arr = jnp.full((1,), core, jnp.int32)
        piece = D // ways

        def grown(value, axis, size, place, dim):
            if size == 1:
                return jnp.expand_dims(value, dim)
            return placed(
                [value] + [ahead(value, axis, size, s) for s in range(1, size)], place, dim
            )

        def spread_z(shard):
            return grown(shard, "z", z_n, z, 0)

        def spread_x(value, x_first):
            return grown(value, both_x, x_n, x, 1 if x_first else 2)

        def spread_y(value):
            return grown(value, "y", y_n, y, 0)

        def spread_core(value):
            value = grown(value, "core", 2, core, 1)
            return value.reshape(ways * value.shape[-2], value.shape[-1])

        def shard_a(layer):
            return jnp.concatenate(
                [qkv_w[layer].transpose(1, 0, 2).reshape(piece, 3 * D), out_w[layer]], axis=1
            ).astype(BF)

        def shard_mlp(layer):
            up = up_w[layer].astype(BF).reshape(piece, ways, 4, piece).swapaxes(1, 2)
            down = down_w[layer].astype(BF).reshape(4, piece, D).swapaxes(0, 1)
            return jnp.concatenate([up.reshape(piece, FF), down.reshape(piece, FF)], axis=1)

        def gather_mlp(shard):
            return lax.all_gather(shard, every, axis=0, tiled=True)

        def along_seqs(blocks):
            return lax.all_to_all(blocks, ("z", "xh"), split_axis=0, concat_axis=0, tiled=True)

        def parts_of(source):
            by_seq = source.transpose(1, 0, 2)
            return [
                lax.dynamic_index_in_dim(by_seq, (chip // 2 + t) % half, 0, keepdims=False)
                for t in range(half)
            ]

        def come(parts):
            return [lax.ppermute(p, every[1:], route) for p, route in zip(parts, routes)]

        def own_rows(got):
            return placed(got[:1] + got[:0:-1], seq_id, 0).reshape(half * lb, D)

        def leave(rows):
            blocks = rows.reshape(half // 2, 2, lb, D)
            got = [
                lax.ppermute(blocks[:, odd], ("core", "xl"), [(b, a) for a, b in turn(odd)])
                for odd in range(2)
            ]
            return along_seqs(jnp.stack(got, axis=1).reshape(half, lb, D))

        def arrived(got):
            return got.transpose(1, 0, 2)

        def leave_at_once(rows):
            got = []
            for t in range(half):
                sent = lax.dynamic_slice(rows, (((seq_id - t) % half) * lb, 0), (lb, D))
                got.append(lax.ppermute(sent, every[1:], [(b, a) for a, b in routes[t]]))
            return got

        gains_row = jnp.pad(vectors.T, ((0, 0), (0, 128 - 5))).astype(BF)
        x_parts = parts_of(tokens)
        chips_a = jnp.concatenate([shard_a(0), gains_row], axis=1)
        chips_a = spread_z(after(chips_a, *x_parts))
        mlp0 = gather_mlp(after(shard_mlp(0), chips_a))
        chips_a = spread_x(chips_a, True)
        own_x = own_rows(come(x_parts))
        next_mlp = shard_mlp(1)
        chips_b = spread_z(after(shard_a(1), own_x))
        chips_a = after(spread_y(after(chips_a, own_x, next_mlp)), chips_b)
        meta = jnp.concatenate([picked_ids, lengths[:, None]], axis=1)
        meta = lax.dynamic_index_in_dim(
            jnp.where(group == core, meta, swap_core(meta)), seq_id, 0, keepdims=False
        )
        picks, length = meta[:-1], meta[-1]
        row_ids = jnp.arange(half * lb, dtype=jnp.int32)
        block = row_ids // lb
        places = (2 * block + ((core + block) & 1)) * lb + row_ids % lb
        chosen = (picks[:, None] == places[None, :]).astype(BF)
        live = (places < length).astype(F32)[:, None]

        def at_picks(rows):
            part = dotf(chosen, rows, NN).astype(BF)
            return part + swap_core(part)

        def to_rows(values):
            return dotf(chosen, values, TN)

        x_low = at_picks(own_x)
        full_a = spread_core(after(chips_a, x_low))
        gains = full_a[:, 4 * D : 4 * D + 5].T.astype(F32)
        chips_b = spread_y(chips_b)
        mlp1 = gather_mlp(after(next_mlp, full_a))
        x_rows = x_low.astype(F32)
        gate = jax.nn.sigmoid(jnp.sum(x_rows * gains[2], axis=-1, keepdims=True))
        n1_0, kv0 = forward_first(x_rows, gains[0], full_a)
        q0 = dotf(n1_0, full_a[:, :D], NN).astype(BF)
        chips_b = spread_x(after(chips_b, q0), False)
        own0 = ((q0, 0), (kv0, 0), (kv0, 6))
        o0, lse0 = attend(*own0, (), core_arr, lb)
        branch0, mid0, n2_0 = forward_second(x_rows, gains[1], full_a, o0)
        mlp0 = (mlp0, mlp0, FF // D)
        act0, slope0, out0 = mlp_forward(n2_0, mlp0)
        both0 = branch0 + out0
        delta = (gate * both0).astype(BF)
        mixed = own_x.astype(F32) + to_rows(delta)

        full_b = spread_core(after(chips_b, n2_0))
        cot_sent = come(parts_of(after(cotangent, full_b)))
        n1_1, kv1 = forward_first(mixed, gains[3], full_b)
        far = swap_core(kv1)
        far1 = ((far, 0), (far, 6))
        q1 = dotf(n1_1, full_b[:, :D], NN).astype(BF)
        own1 = ((q1, 0), (kv1, 0), (kv1, 6))
        o1, lse1 = attend(*own1, far1, core_arr, lb)
        branch1, mid1, n2_1 = forward_second(mixed, gains[4], full_b, o1)
        mlp1 = (mlp1, mlp1, FF // D)
        act1, slope1, out1 = mlp_forward(n2_1, mlp1)
        act_rows = (live * (mid1 + out1)).astype(BF)
        act_sent = leave(act_rows)
        d_top = live * own_rows([after(c, n2_1) for c in cot_sent]).astype(F32)

        def by_shard(grad):
            return grad.reshape(y_n, 2, z_n, x_n, grad.shape[0] // ways, grad.shape[1])

        def at(grads, which, dim):
            return jnp.concatenate(
                [lax.dynamic_index_in_dim(g, which, dim, keepdims=False) for g in grads], axis=-1
            )

        def over_core(*grads):
            grads = [by_shard(g) for g in grads]
            got = swap_core(at(grads, 1 - core, 1))
            return (at(grads, core, 1).astype(F32) + got.astype(F32)).astype(BF)

        def of_core(*grads):
            return at([by_shard(g) for g in grads], core, 1)

        class Sum:
            def __init__(self, value, axis, dim):
                size, place = (y_n, y) if axis == "y" else (x_n, x)
                self.own = at([value], place, dim)
                self.cut = [at([value], (place + size - s) % size, dim) for s in range(1, size)]
                self.got = [ahead(c, axis, size, s + 1) for s, c in enumerate(self.cut)]

            def done(self, *late):
                total = self.own.astype(F32)
                for got in self.got:
                    total = total + after(got, *late).astype(F32)
                return total.astype(BF)

        class LastSum:
            def __init__(self, *values):
                whole = jnp.concatenate(values, axis=-1)
                self.own = at([whole], z, 0)
                self.cut = [at([whole], (z + z_n - s) % z_n, 0) for s in range(1, z_n)]
                self.got = [ahead(c, "z", z_n, s + 1) for s, c in enumerate(self.cut)]

            def done(self, *late):
                total = self.own.astype(F32)
                for got in self.got:
                    total = total + after(got, *late).astype(F32)
                return total

        def first_way(value, x_first):
            return Sum(value, both_x, 2) if x_first else Sum(value, "y", 0)

        def second_way(value, x_first):
            return Sum(value, "y", 0) if x_first else Sum(value, both_x, 1)

        def columns(*vectors):
            return jnp.pad(jnp.stack(vectors, 1), ((0, 0), (0, 128 - len(vectors)))).astype(BF)

        d_mid1, do1, g_out1, g_up1, g_down1, g_b1 = back_mlp(
            mid1, (full_b, mlp1), gains[4], (o1, n2_1, act1, slope1),
            after(d_top.astype(BF), act_rows), d_top, None
        )
        up1, down1 = over_core(g_up1), over_core(g_down1)
        up1, down1 = first_way(up1, False), first_way(down1, True)
        do1 = after(do1, *up1.cut, *down1.cut)
        parts = []
        for first, count in ((0, 4), (4, 2)):
            dq, d_own, d_far = attend_back(
                own1[0], (do1, 0), (o1, 0), lse1, own1[1], own1[2], far1, core_arr, lb, first, count
            )
            parts.append((dq, d_own, swap_core(d_far)))
            up1, down1 = up1.done(dq), down1.done(dq)
            if first == 0:
                up1, down1 = second_way(up1, False), second_way(down1, True)
                act_sent = after(act_sent, dq)
                do1 = after(do1, dq, act_sent, *up1.cut, *down1.cut)
        pair1 = LastSum(up1, down1)
        d_q1 = jnp.concatenate([parts[0][0], dq], axis=1)
        sums = [(d_own + back.astype(F32)).astype(BF) for _, d_own, back in parts]
        d_kv1 = jnp.concatenate([s[0] for s in sums] + [s[1] for s in sums], axis=1)
        d_mixed, g_q1, g_kv1, g_a1 = back_qkv(mixed, full_b, gains[3], n1_1, d_q1, d_kv1, d_mid1)
        head1 = over_core(g_q1, g_kv1, g_out1, columns(g_a1, g_b1))

        d_delta = at_picks(d_mixed.astype(BF)).astype(F32)
        gated = gate * d_delta
        d_logit = gate * (1.0 - gate) * jnp.sum(d_delta * both0, axis=-1, keepdims=True)
        head1a = first_way(head1[..., : 2 * D], False)
        head1b = first_way(head1[..., 2 * D :], True)
        gated_low = after(gated.astype(BF), *head1a.cut, *head1b.cut)
        d_mid0, do0, g_out0, g_up0, g_down0, g_b0 = back_mlp(
            mid0, (full_a, mlp0), gains[1], (o0, n2_0, act0, slope0), gated_low, None, gated
        )
        up0, down0 = first_way(of_core(g_up0), False), first_way(of_core(g_down0), True)
        head1a = second_way(head1a.done(d_mid0), False)
        head1b = second_way(head1b.done(d_mid0), True)
        do0 = after(do0, *up0.cut, *down0.cut, *head1a.cut, *head1b.cut, *pair1.got)
        dq, d_kv = attend_back(
            own0[0], (do0, 0), (o0, 0), lse0, own0[1], own0[2], (), core_arr, lb, 0, PAIRS
        )
        d_kv0 = jnp.concatenate([d_kv[0], d_kv[1]], axis=1)
        d_rows0, g_q0, g_kv0, g_a0 = back_qkv(x_rows, full_a, gains[0], n1_0, dq, d_kv0, d_mid0)
        g_r = jnp.sum(d_logit * x_rows, axis=0)
        d_chosen = (d_rows0 + d_logit * gains[2]).astype(BF)
        grad_rows = (d_mixed + to_rows(d_chosen)).astype(BF)
        grad_sent = leave_at_once(grad_rows)
        head1a, head1b = head1a.done(grad_rows), head1b.done(grad_rows)
        up0, down0 = up0.done(grad_rows), down0.done(grad_rows)
        up0, down0 = second_way(up0, False), second_way(down0, True)
        head0a = after(of_core(g_q0, g_kv0[:, :D]), *up0.cut, *down0.cut)
        head0b = of_core(g_kv0[:, D:], g_out0, columns(g_a0, g_b0, g_r))
        head0b = after(head0b, *up0.cut, *down0.cut)
        head0a, head0b = first_way(head0a, False), first_way(head0b, True)
        up0, down0 = up0.done(*head0a.cut, *head0b.cut), down0.done(*head0a.cut, *head0b.cut)
        early = LastSum(up0, down0, head1a, head1b)
        grad_sent = [after(g, *early.cut) for g in grad_sent]
        input_grad = arrived(placed(grad_sent, chip // 2, 0)).astype(F32)
        activations = arrived(after(act_sent, *early.cut))
        head0a, head0b = head0a.done(*early.cut), head0b.done(*early.cut)
        pair1 = pair1.done(*early.cut)
        head0a, head0b = second_way(head0a, False), second_way(head0b, True)
        head0 = LastSum(head0a.done(), head0b.done())
        early = early.done(*head0.cut)
        head0 = head0.done(early)
        squares = sum(jnp.sum(v * v) for v in (early, head0, pair1))
        up0, down0, head1 = early[:, :FF], early[:, FF : 2 * FF], early[:, 2 * FF :]
        up1, down1 = pair1[:, :FF], pair1[:, FF:]

        def unmixed(up):
            return up.reshape(piece, 4, ways, piece).swapaxes(1, 2).reshape(piece, FF)

        def unpacked(down):
            return down.reshape(piece, 4, D).swapaxes(0, 1).reshape(4 * piece, D)

        shards = [
            jnp.stack([h[:, : 3 * D].reshape(piece, 3, D).transpose(1, 0, 2) for h in (head0, head1)]),
            jnp.stack([head0[:, 3 * D : 4 * D], head1[:, 3 * D : 4 * D]]),
            jnp.stack([unmixed(up0), unmixed(up1)]),
            jnp.stack([unpacked(down0), unpacked(down1)]),
            jnp.concatenate([head0[:, 4 * D : 4 * D + 3].T, head1[:, 4 * D : 4 * D + 2].T]),
        ]
        grad_norm = jnp.sqrt(all_sum(squares.reshape(1, 1))[0, 0])
        factor = 1.0 / jnp.maximum(grad_norm, 1.0)
        base_rate = math.sqrt(NPARAMS / D)
        rates = (base_rate, math.sqrt(NPARAMS * LEN / (8 * D)), base_rate, base_rate, base_rate)
        masters = (qkv_w, out_w, up_w, down_w, vectors)
        moms = (qkv_mom, out_mom, up_mom, down_mom, vec_mom)
        avgs = (qkv_avg, out_avg, up_avg, down_avg, vec_avg)
        new_w, new_m, new_z = [], [], []
        for weight, grad, mom, avg, rate in zip(masters, shards, moms, avgs, rates):
            clipped = grad * factor
            m = 0.5 * mom + clipped
            w = weight - rate * (clipped + 0.5 * m)
            new_w.append(w)
            new_m.append(m)
            new_z.append(0.5 * avg + 0.5 * w)
        return (activations, input_grad, grad_norm, *new_w, *new_m, *new_z)

    group_spec = ("y", "core")
    pos_spec = ("z", "xh", "xl")
    rows_spec = P(pos_spec, group_spec, None)
    param_specs = (
        P(None, None, every, None),
        P(None, every, None),
        P(None, every, None),
        P(None, every, None),
        P(None, every),
    )
    return jax.shard_map(
        body,
        mesh=inner,
        in_specs=(rows_spec, rows_spec, P(group_spec, None), P(group_spec)) + param_specs * 3,
        out_specs=(rows_spec, rows_spec, P()) + param_specs * 3,
        check_vma=False,
    )
```

```python
import functools
import math

import jax
import jax.numpy as jnp
from jax import lax
from jax.experimental import pallas as pl
from jax.experimental.pallas import tpu as pltpu
from jax.sharding import Mesh
from jax.sharding import PartitionSpec as P

D = 768
FF = 3072
LEN = 2048
NPARAMS = 14159616
EPS = 1e-06
PAIRS = 6
TQ = 256
NN = (((1,), (0,)), ((), ()))
NT = (((1,), (1,)), ((), ()))
TN = (((0,), (0,)), ((), ()))
BF = jnp.bfloat16
F32 = jnp.float32


def dotf(left, right, dims):
    return lax.dot_general(left, right, dims, preferred_element_type=F32)


def far_mask(core, tile, lb, q_axis):
    shift = lb.bit_length() - 1
    iq = lax.broadcasted_iota(jnp.int32, (TQ, TQ), q_axis) >> shift
    ik = lax.broadcasted_iota(jnp.int32, (TQ, TQ), 1 - q_axis) >> shift
    odd = (core + tile * (TQ >> shift) + iq) & 1
    return (iq > ik) | ((iq == ik) & (odd == 1))


def attend_kernel(lb, core_ref, *refs):
    if lb:
        q_ref, ko, vo, kf, vf, o_ref, lse_ref = refs
    else:
        q_ref, ko, vo, o_ref, lse_ref = refs
    rows = q_ref.shape[0]
    lane = lax.broadcasted_iota(jnp.int32, (TQ, 128), 1)
    tri = lax.broadcasted_iota(jnp.int32, (TQ, TQ), 0) >= lax.broadcasted_iota(
        jnp.int32, (TQ, TQ), 1
    )
    for t in range(rows // TQ):
        n = t * TQ
        q = q_ref[pl.ds(n, TQ), :] * BF(0.125)
        outs = []
        cols = []
        if lb:
            fm = far_mask(core_ref[0], t, lb, 0)
        for h in range(2):
            qm = jnp.where((lane >= 64) if h else (lane < 64), q, BF(0))
            segs = []
            if t:
                segs.append((dotf(qm, ko[pl.ds(0, n), :], NT), vo[pl.ds(0, n), :]))
            segs.append(
                (jnp.where(tri, dotf(qm, ko[pl.ds(n, TQ), :], NT), -1e30), vo[pl.ds(n, TQ), :])
            )
            if lb:
                if t:
                    segs.append((dotf(qm, kf[pl.ds(0, n), :], NT), vf[pl.ds(0, n), :]))
                segs.append(
                    (jnp.where(fm, dotf(qm, kf[pl.ds(n, TQ), :], NT), -1e30), vf[pl.ds(n, TQ), :])
                )
            top = functools.reduce(
                jnp.maximum, [jnp.max(s, axis=1, keepdims=True) for s, _ in segs]
            )
            total = 0.0
            acc = 0.0
            for s, v in segs:
                e = jnp.exp(s - top)
                total = total + jnp.sum(e, axis=1, keepdims=True)
                acc = acc + dotf(e.astype(BF), v, NN)
            outs.append(acc * (1.0 / total))
            cols.append(jnp.broadcast_to(top + jnp.log(total), (TQ, 128)))
        o_ref[pl.ds(n, TQ), :] = jnp.where(lane < 64, outs[0], outs[1]).astype(BF)
        for h in range(2):
            lse_ref[0, pl.ds(h, 1), pl.ds(n, TQ)] = cols[h].T[0:1, :]


def attend(q, k_own, v_own, far, core, lb):
    rows = q[0].shape[0]
    ops = [q, k_own, v_own] + list(far)

    def spec(off):
        return pl.BlockSpec((rows, 128), lambda i, off=off: (0, off + i))

    size = 12 * rows * rows * (1 if far else 0.5)
    return pl.pallas_call(
        functools.partial(attend_kernel, lb if far else 0),
        grid=(PAIRS,),
        in_specs=[pl.BlockSpec(memory_space=pltpu.SMEM)] + [spec(o) for _, o in ops],
        out_specs=[spec(0), pl.BlockSpec((1, 2, rows), lambda i: (i, 0, 0))],
        out_shape=[
            jax.ShapeDtypeStruct((rows, D), BF),
            jax.ShapeDtypeStruct((PAIRS, 2, rows), F32),
        ],
        compiler_params=pltpu.CompilerParams(vmem_limit_bytes=40 * 2**20),
        cost_estimate=pl.CostEstimate(
            flops=int(4 * 64 * 6 * size), bytes_accessed=rows * D * 12, transcendentals=int(size)
        ),
        name="attend_far" if far else "attend_own",
    )(core, *[a for a, _ in ops])


def attend_back_kernel(lb, kc, core_ref, *refs):
    if lb:
        q_ref, do_ref, o_ref, lse_ref, ko, vo, kf, vf = refs[:8]
        dq_ref, d_own, d_far, k_t, aok, aov, afk, afv = refs[8:]
        parts = [(ko, vo, aok, aov, 0), (kf, vf, afk, afv, 1)]
    else:
        q_ref, do_ref, o_ref, lse_ref, ko, vo, dq_ref, d_own, k_t, aok, aov = refs
        parts = [(ko, vo, aok, aov, 0)]
    rows = q_ref.shape[0]
    lane = lax.broadcasted_iota(jnp.int32, (TQ, 128), 1)
    tri = lax.broadcasted_iota(jnp.int32, (TQ, TQ), 1) >= lax.broadcasted_iota(
        jnp.int32, (TQ, TQ), 0
    )
    for k, _, ak, av, s in parts:
        k_t[s] = k[...].astype(F32).T.astype(BF)
        ak[...] = jnp.zeros_like(ak)
        av[...] = jnp.zeros_like(av)
    for t in range(rows // TQ):
        n = t * TQ
        q = q_ref[pl.ds(n, TQ), :] * BF(0.125)
        do = do_ref[pl.ds(n, TQ), :]
        prod = (do.astype(F32) * o_ref[pl.ds(n, TQ), :].astype(F32)).T
        dqs = []
        if lb:
            fm = far_mask(core_ref[0], t, lb, 1)
        for h in range(2):
            half = (lane >= 64) if h else (lane < 64)
            qm = jnp.where(half, q, BF(0))
            dom = jnp.where(half, do, BF(0))
            inner = jnp.sum(prod[64 * h : 64 * h + 64], axis=0, keepdims=True)
            lse = lse_ref[0, pl.ds(h, 1), pl.ds(n, TQ)]
            dq_t = 0.0
            for k, v, ak, av, s in parts:
                spans = []
                a = 0
                while a < n:
                    w = min(kc, n - a)
                    spans.append((a, w, None))
                    a += w
                spans.append((n, TQ, fm if s else tri))
                for a, w, mask in spans:
                    p = jnp.exp(dotf(k[pl.ds(a, w), :], qm, NT) - lse)
                    if mask is not None:
                        p = jnp.where(mask, p, 0.0)
                    dp = dotf(v[pl.ds(a, w), :], dom, NT)
                    ds = (p * (dp - inner)).astype(BF)
                    av[pl.ds(a, w), :] += dotf(p.astype(BF), dom, NN)
                    ak[pl.ds(a, w), :] += dotf(ds, qm, NN)
                    dq_t = dq_t + dotf(k_t[s, 64 * h : 64 * h + 64, a : a + w], ds, NN)
            dqs.append(dq_t)
        dq_ref[pl.ds(n, TQ), :] = (jnp.concatenate(dqs, axis=0) * 0.125).T.astype(BF)
    d_own[0] = aok[...].astype(d_own.dtype)
    d_own[1] = aov[...].astype(d_own.dtype)
    if lb:
        d_far[0] = afk[...].astype(BF)
        d_far[1] = afv[...].astype(BF)


def attend_back(q, do, o, lse, k_own, v_own, far, core, lb, first, count, kc=1024):
    rows = do[0].shape[0]

    def spec(off):
        return pl.BlockSpec((rows, 128), lambda i, off=off: (0, off + i))

    two = pl.BlockSpec((2, rows, 128), lambda i: (0, 0, i))
    lse_spec = pl.BlockSpec((1, 2, rows), lambda i: (i + first, 0, 0))
    ops = [q, do, o, None, k_own, v_own] + list(far)
    wide = count * 128
    outs = [
        jax.ShapeDtypeStruct((rows, wide), BF),
        jax.ShapeDtypeStruct((2, rows, wide), F32 if far else BF),
    ]
    if far:
        outs.append(jax.ShapeDtypeStruct((2, rows, wide), BF))
    size = 2 * count * rows * rows * (1 if far else 0.5)
    return pl.pallas_call(
        functools.partial(attend_back_kernel, lb if far else 0, kc),
        grid=(count,),
        in_specs=[pl.BlockSpec(memory_space=pltpu.SMEM)]
        + [lse_spec if e is None else spec(e[1] + first) for e in ops],
        out_specs=[spec(0)] + [two] * (len(outs) - 1),
        out_shape=outs,
        scratch_shapes=[pltpu.VMEM((2 if far else 1, 128, rows), BF)]
        + [pltpu.VMEM((rows, 128), F32)] * (4 if far else 2),
        compiler_params=pltpu.CompilerParams(vmem_limit_bytes=40 * 2**20),
        cost_estimate=pl.CostEstimate(
            flops=int(10 * 64 * 5 * size), bytes_accessed=rows * D * 24, transcendentals=int(size)
        ),
        name="attend_back_far" if far else "attend_back_own",
    )(core, *[lse if e is None else e[0] for e in ops])


def place_kernel(count, start_ref, *refs):
    out = refs[count]
    for s in range(count):
        at = start_ref[0] + s
        out[0, jnp.where(at >= count, at - count, at)] = refs[s][0]


def placed(parts, start, dim):
    count = len(parts)
    shape = parts[0].shape
    r, c = shape[-2:]
    g = math.prod(shape[:dim])
    h = math.prod(shape[dim:-2])
    cut = h
    while cut % 2 == 0 and cut * r * c * count > 2**20:
        cut //= 2
    got = pl.pallas_call(
        functools.partial(place_kernel, count),
        grid=(g, h // cut),
        in_specs=[pl.BlockSpec(memory_space=pltpu.SMEM)]
        + [pl.BlockSpec((1, cut, r, c), lambda i, j: (i, j, 0, 0))] * count,
        out_specs=pl.BlockSpec((1, count, cut, r, c), lambda i, j: (i, 0, j, 0, 0)),
        out_shape=jax.ShapeDtypeStruct((g, count, h, r, c), parts[0].dtype),
        compiler_params=pltpu.CompilerParams(vmem_limit_bytes=32 * 2**20),
        cost_estimate=pl.CostEstimate(
            flops=0, bytes_accessed=4 * count * math.prod(shape), transcendentals=0
        ),
        name="place",
    )(start.reshape(1).astype(jnp.int32), *[p.reshape(g, h, r, c) for p in parts])
    return got.reshape(shape[:dim] + (count,) + shape[dim:])


def mlp_kernel(n2_ref, up_ref, down_ref, act_ref, slope_ref, mlp_ref):
    rows = n2_ref.shape[0]

    @pl.when(pl.program_id(0) == 0)
    def _():
        mlp_ref[...] = jnp.zeros_like(mlp_ref)

    for t in range(rows // TQ):
        part = pl.ds(t * TQ, TQ)
        act, slope = gelu_parts(dotf(n2_ref[part, :], up_ref[...], NN))
        act_ref[part, :] = act
        slope_ref[part, :] = slope
        mlp_ref[part, :] += dotf(act, down_ref[...], NN)


def up_spec(wide):
    return pl.BlockSpec((D, wide), lambda i: (0, i))


def down_spec(wide, first=0):
    cuts = D // wide
    return pl.BlockSpec((wide, D), lambda i: (i % cuts, first + i // cuts))


def mlp_forward(n2, w_mlp, wide=768):
    rows = n2.shape[0]
    whole = pl.BlockSpec((rows, D), lambda i: (0, 0))
    across = pl.BlockSpec((rows, wide), lambda i: (0, i))
    return pl.pallas_call(
        mlp_kernel,
        grid=(FF // wide,),
        in_specs=[whole, up_spec(wide), down_spec(wide, w_mlp[2])],
        out_specs=[across, across, whole],
        out_shape=[
            jax.ShapeDtypeStruct((rows, FF), BF),
            jax.ShapeDtypeStruct((rows, FF), BF),
            jax.ShapeDtypeStruct((rows, D), F32),
        ],
        compiler_params=pltpu.CompilerParams(vmem_limit_bytes=56 * 2**20),
        cost_estimate=pl.CostEstimate(
            flops=4 * rows * D * FF,
            bytes_accessed=4 * rows * FF + 4 * D * FF + 6 * rows * D,
            transcendentals=rows * FF,
        ),
        name="mlp_forward",
    )(n2, w_mlp[0], w_mlp[1])


def mlp_back_kernel(
    dm_ref, n2_ref, act_ref, slope_ref, up_ref, down_ref, gu_ref, gd_ref, dn_ref, dm_t, n2_t, pre
):
    rows = dm_ref.shape[0]

    @pl.when(pl.program_id(0) == 0)
    def _():
        dm_t[...] = dm_ref[...].astype(F32).T.astype(BF)
        n2_t[...] = n2_ref[...].astype(F32).T.astype(BF)
        dn_ref[...] = jnp.zeros_like(dn_ref)

    for t in range(rows // TQ):
        part = pl.ds(t * TQ, TQ)
        d_act = dotf(dm_ref[part, :], down_ref[...], NT)
        d_pre = (slope_ref[part, :].astype(F32) * d_act).astype(BF)
        pre[part, :] = d_pre
        dn_ref[part, :] += dotf(d_pre, up_ref[...], NT)
    gu_ref[...] = dotf(n2_t[...], pre[...], NN).astype(BF)
    gd_ref[...] = dotf(dm_t[...], act_ref[...], NN).T.astype(BF)


def mlp_backward(d_mlp, n2, act, slope, w_mlp, wide=768):
    rows = n2.shape[0]
    whole = pl.BlockSpec((rows, D), lambda i: (0, 0))
    across = pl.BlockSpec((rows, wide), lambda i: (0, i))
    return pl.pallas_call(
        mlp_back_kernel,
        grid=(FF // wide,),
        in_specs=[whole, whole, across, across, up_spec(wide), down_spec(wide, w_mlp[2])],
        out_specs=[up_spec(wide), down_spec(wide), whole],
        out_shape=[
            jax.ShapeDtypeStruct((D, FF), BF),
            jax.ShapeDtypeStruct((D, FF), BF),
            jax.ShapeDtypeStruct((rows, D), F32),
        ],
        scratch_shapes=[
            pltpu.VMEM((D, rows), BF),
            pltpu.VMEM((D, rows), BF),
            pltpu.VMEM((rows, wide), BF),
        ],
        compiler_params=pltpu.CompilerParams(vmem_limit_bytes=56 * 2**20),
        cost_estimate=pl.CostEstimate(
            flops=8 * rows * D * FF,
            bytes_accessed=4 * rows * FF + 8 * D * FF + 8 * rows * D,
            transcendentals=0,
        ),
        name="mlp_backward",
    )(d_mlp, n2, act, slope, w_mlp[0], w_mlp[1])


def norm_parts(rows):
    scale = lax.rsqrt(jnp.mean(rows * rows, axis=-1, keepdims=True) + EPS)
    return rows * scale, scale


def norm_back(d_out, unit, scale, gain):
    d_gain = jnp.sum(d_out * unit, axis=0)
    d_unit = d_out * gain
    d_rows = scale * (d_unit - unit * jnp.mean(d_unit * unit, axis=-1, keepdims=True))
    return d_rows, d_gain


def gelu_parts(pre):
    c = math.sqrt(2.0 / math.pi)
    k = 0.044715 * c
    sq = pre * pre
    h = 0.5 * jnp.tanh(pre * (c + k * sq)) + 0.5
    act = pre * h
    slope = h + (act * (1.0 - h)) * (2.0 * c + (6.0 * k) * sq)
    return act.astype(BF), slope.astype(BF)


def after(value, *others):
    return lax.optimization_barrier((value, *others))[0]


def forward_first(rows, gain_a, w_a):
    unit_a, _ = norm_parts(rows)
    n1 = (unit_a * gain_a).astype(BF)
    return n1, dotf(n1, w_a[:, D : 3 * D], NN).astype(BF)


def forward_second(rows, gain_b, w_a, o):
    branch = dotf(o, w_a[:, 3 * D : 4 * D], NN)
    mid = rows + branch
    unit_b, _ = norm_parts(mid)
    return branch, mid, (unit_b * gain_b).astype(BF)


def back_mlp(mid, weights, gain_b, saved, mlp_low, d_top, d_extra):
    o, n2, act, slope = saved
    w_a, w_mlp = weights
    g_up, g_down, d_n2 = mlp_backward(mlp_low, n2, act, slope, w_mlp)
    unit_b, scale_b = norm_parts(mid)
    d_mid, g_b = norm_back(d_n2, unit_b, scale_b, gain_b)
    if d_top is not None:
        d_mid = d_mid + d_top
    d_branch = (d_mid if d_extra is None else d_mid + d_extra).astype(BF)
    do = dotf(d_branch, w_a[:, 3 * D : 4 * D], NT).astype(BF)
    g_out = dotf(o, d_branch, TN).astype(BF)
    return d_mid, do, g_out, g_up, g_down, g_b


def back_qkv(rows, w_a, gain_a, n1, d_q, d_kv, d_mid):
    g_q = dotf(n1, d_q, TN).astype(BF)
    g_kv = dotf(n1, d_kv, TN).astype(BF)
    unit_a, scale_a = norm_parts(rows)
    d_n1 = dotf(d_q, w_a[:, :D], NT) + dotf(d_kv, w_a[:, D : 3 * D], NT)
    d_rows, g_a = norm_back(d_n1, unit_a, scale_a, gain_a)
    return d_rows + d_mid, g_q, g_kv, g_a


def ahead(value, axis, size, step):
    return lax.ppermute(value, axis, [(i, (i - step) % size) for i in range(size)])


def solution(mesh):
    dp, seq = mesh.shape["dp"], mesh.shape["seq"]
    y_n = dp // 2
    x_n = y_n if seq % y_n == 0 else 1
    z_n = seq // x_n
    half = seq // 2
    ways = dp * seq
    inner = Mesh(
        mesh.devices.reshape(y_n, 2, z_n, x_n // 2, 2), ("y", "core", "z", "xh", "xl")
    )
    both_x = ("xh", "xl")
    every = ("y", "core", "z", "xh", "xl")
    lb = LEN // seq

    def route(t):
        pairs = []
        for c in range(2):
            for s in range(seq):
                block = s // 2
                pairs.append((c * seq + s, ((s ^ block) & 1) * seq + 2 * ((block + t) % half) + c))
        return pairs

    routes = [route(t) for t in range(half)]

    def turn(odd):
        return [(c * 2 + e, (e ^ odd) * 2 + c) for c in range(2) for e in range(2)]

    def swap_core(value):
        return lax.ppermute(value, "core", [(0, 1), (1, 0)])

    def all_sum(value):
        pair = [
            lax.ppermute(
                value,
                ("core", *both_x),
                [
                    (c * x_n + i, ((c + dc) % 2) * x_n + (i + dx) % x_n)
                    for c in range(2)
                    for i in range(x_n)
                ],
            )
            for dc in range(2)
            for dx in range(x_n)
            if dc or dx
        ]
        value = sum(pair, start=value)
        for axis, size in (("y", y_n), ("z", z_n)):
            value = sum(
                (ahead(value, axis, size, s) for s in range(1, size)), start=value
            )
        return value

    def body(
        tokens, cotangent, picked_ids, lengths,
        qkv_w, out_w, up_w, down_w, vectors,
        qkv_mom, out_mom, up_mom, down_mom, vec_mom,
        qkv_avg, out_avg, up_avg, down_avg, vec_avg,
    ):
        y, core, z, x = (lax.axis_index(a) for a in ("y", "core", "z", both_x))
        chip = z * x_n + x
        seq_id = chip // 2
        group = chip % 2
        core_arr = jnp.full((1,), core, jnp.int32)
        piece = D // ways

        def grown(value, axis, size, place, dim):
            if size == 1:
                return jnp.expand_dims(value, dim)
            return placed(
                [value] + [ahead(value, axis, size, s) for s in range(1, size)], place, dim
            )

        def spread_z(shard):
            return grown(shard, "z", z_n, z, 0)

        def spread_x(value, x_first):
            return grown(value, both_x, x_n, x, 1 if x_first else 2)

        def spread_y(value):
            return grown(value, "y", y_n, y, 0)

        def spread_core(value):
            value = grown(value, "core", 2, core, 1)
            return value.reshape(ways * value.shape[-2], value.shape[-1])

        def shard_a(layer):
            return jnp.concatenate(
                [qkv_w[layer].transpose(1, 0, 2).reshape(piece, 3 * D), out_w[layer]], axis=1
            ).astype(BF)

        def shard_mlp(layer):
            up = up_w[layer].astype(BF).reshape(piece, ways, 4, piece).swapaxes(1, 2)
            down = down_w[layer].astype(BF).reshape(4, piece, D).swapaxes(0, 1)
            return jnp.concatenate([up.reshape(piece, FF), down.reshape(piece, FF)], axis=1)

        def gather_mlp(shard):
            return lax.all_gather(shard, every, axis=0, tiled=True)

        def along_seqs(blocks):
            return lax.all_to_all(blocks, ("z", "xh"), split_axis=0, concat_axis=0, tiled=True)

        def parts_of(source):
            by_seq = source.transpose(1, 0, 2)
            return [
                lax.dynamic_index_in_dim(by_seq, (chip // 2 + t) % half, 0, keepdims=False)
                for t in range(half)
            ]

        def come(parts):
            return [lax.ppermute(p, every[1:], route) for p, route in zip(parts, routes)]

        def own_rows(got):
            return placed(got[:1] + got[:0:-1], seq_id, 0).reshape(half * lb, D)

        def leave(rows):
            blocks = rows.reshape(half // 2, 2, lb, D)
            got = [
                lax.ppermute(blocks[:, odd], ("core", "xl"), [(b, a) for a, b in turn(odd)])
                for odd in range(2)
            ]
            return along_seqs(jnp.stack(got, axis=1).reshape(half, lb, D))

        def arrived(got):
            return got.transpose(1, 0, 2)

        def leave_at_once(rows):
            got = []
            for t in range(half):
                sent = lax.dynamic_slice(rows, (((seq_id - t) % half) * lb, 0), (lb, D))
                got.append(lax.ppermute(sent, every[1:], [(b, a) for a, b in routes[t]]))
            return got

        gains_row = jnp.pad(vectors.T, ((0, 0), (0, 128 - 5))).astype(BF)
        x_parts = parts_of(tokens)
        chips_a = jnp.concatenate([shard_a(0), gains_row], axis=1)
        chips_a = spread_z(after(chips_a, *x_parts))
        mlp0 = gather_mlp(after(shard_mlp(0), chips_a))
        chips_a = spread_x(chips_a, True)
        own_x = own_rows(come(x_parts))
        next_mlp = shard_mlp(1)
        chips_b = spread_z(after(shard_a(1), own_x))
        chips_a = after(spread_y(after(chips_a, own_x, next_mlp)), chips_b)
        meta = jnp.concatenate([picked_ids, lengths[:, None]], axis=1)
        meta = lax.dynamic_index_in_dim(
            jnp.where(group == core, meta, swap_core(meta)), seq_id, 0, keepdims=False
        )
        picks, length = meta[:-1], meta[-1]
        row_ids = jnp.arange(half * lb, dtype=jnp.int32)
        block = row_ids // lb
        places = (2 * block + ((core + block) & 1)) * lb + row_ids % lb
        chosen = (picks[:, None] == places[None, :]).astype(BF)
        live = (places < length).astype(F32)[:, None]

        def at_picks(rows):
            part = dotf(chosen, rows, NN).astype(BF)
            return part + swap_core(part)

        def to_rows(values):
            return dotf(chosen, values, TN)

        x_low = at_picks(own_x)
        full_a = spread_core(after(chips_a, x_low))
        gains = full_a[:, 4 * D : 4 * D + 5].T.astype(F32)
        chips_b = spread_y(chips_b)
        mlp1 = gather_mlp(after(next_mlp, full_a))
        x_rows = x_low.astype(F32)
        gate = jax.nn.sigmoid(jnp.sum(x_rows * gains[2], axis=-1, keepdims=True))
        n1_0, kv0 = forward_first(x_rows, gains[0], full_a)
        q0 = dotf(n1_0, full_a[:, :D], NN).astype(BF)
        chips_b = spread_x(after(chips_b, q0), False)
        own0 = ((q0, 0), (kv0, 0), (kv0, 6))
        o0, lse0 = attend(*own0, (), core_arr, lb)
        branch0, mid0, n2_0 = forward_second(x_rows, gains[1], full_a, o0)
        mlp0 = (mlp0, mlp0, FF // D)
        act0, slope0, out0 = mlp_forward(n2_0, mlp0)
        both0 = branch0 + out0
        delta = (gate * both0).astype(BF)
        mixed = own_x.astype(F32) + to_rows(delta)

        full_b = spread_core(after(chips_b, n2_0))
        cot_sent = come(parts_of(after(cotangent, full_b)))
        n1_1, kv1 = forward_first(mixed, gains[3], full_b)
        far = swap_core(kv1)
        far1 = ((far, 0), (far, 6))
        q1 = dotf(n1_1, full_b[:, :D], NN).astype(BF)
        own1 = ((q1, 0), (kv1, 0), (kv1, 6))
        o1, lse1 = attend(*own1, far1, core_arr, lb)
        branch1, mid1, n2_1 = forward_second(mixed, gains[4], full_b, o1)
        mlp1 = (mlp1, mlp1, FF // D)
        act1, slope1, out1 = mlp_forward(n2_1, mlp1)
        act_rows = (live * (mid1 + out1)).astype(BF)
        act_sent = leave(act_rows)
        d_top = live * own_rows([after(c, n2_1) for c in cot_sent]).astype(F32)

        def by_shard(grad):
            return grad.reshape(y_n, 2, z_n, x_n, grad.shape[0] // ways, grad.shape[1])

        def at(grads, which, dim):
            return jnp.concatenate(
                [lax.dynamic_index_in_dim(g, which, dim, keepdims=False) for g in grads], axis=-1
            )

        def over_core(*grads):
            grads = [by_shard(g) for g in grads]
            got = swap_core(at(grads, 1 - core, 1))
            return (at(grads, core, 1).astype(F32) + got.astype(F32)).astype(BF)

        def of_core(*grads):
            return at([by_shard(g) for g in grads], core, 1)

        class Sum:
            def __init__(self, value, axis, dim):
                size, place = (y_n, y) if axis == "y" else (x_n, x)
                self.own = at([value], place, dim)
                self.cut = [at([value], (place + size - s) % size, dim) for s in range(1, size)]
                self.got = [ahead(c, axis, size, s + 1) for s, c in enumerate(self.cut)]

            def done(self, *late):
                total = self.own.astype(F32)
                for got in self.got:
                    total = total + after(got, *late).astype(F32)
                return total.astype(BF)

        class LastSum:
            def __init__(self, *values):
                whole = jnp.concatenate(values, axis=-1)
                self.own = at([whole], z, 0)
                self.cut = [at([whole], (z + z_n - s) % z_n, 0) for s in range(1, z_n)]
                self.got = [ahead(c, "z", z_n, s + 1) for s, c in enumerate(self.cut)]

            def done(self, *late):
                total = self.own.astype(F32)
                for got in self.got:
                    total = total + after(got, *late).astype(F32)
                return total

        def first_way(value, x_first):
            return Sum(value, both_x, 2) if x_first else Sum(value, "y", 0)

        def second_way(value, x_first):
            return Sum(value, "y", 0) if x_first else Sum(value, both_x, 1)

        def columns(*vectors):
            return jnp.pad(jnp.stack(vectors, 1), ((0, 0), (0, 128 - len(vectors)))).astype(BF)

        d_mid1, do1, g_out1, g_up1, g_down1, g_b1 = back_mlp(
            mid1, (full_b, mlp1), gains[4], (o1, n2_1, act1, slope1),
            after(d_top.astype(BF), act_rows), d_top, None
        )
        up1, down1 = over_core(g_up1), over_core(g_down1)
        up1, down1 = first_way(up1, False), first_way(down1, True)
        do1 = after(do1, *up1.cut, *down1.cut)
        parts = []
        for first, count in ((0, 4), (4, 2)):
            dq, d_own, d_far = attend_back(
                own1[0], (do1, 0), (o1, 0), lse1, own1[1], own1[2], far1, core_arr, lb, first, count
            )
            parts.append((dq, d_own, swap_core(d_far)))
            up1, down1 = up1.done(dq), down1.done(dq)
            if first == 0:
                up1, down1 = second_way(up1, False), second_way(down1, True)
                act_sent = after(act_sent, dq)
                do1 = after(do1, dq, act_sent, *up1.cut, *down1.cut)
        pair1 = LastSum(up1, down1)
        d_q1 = jnp.concatenate([parts[0][0], dq], axis=1)
        sums = [(d_own + back.astype(F32)).astype(BF) for _, d_own, back in parts]
        d_kv1 = jnp.concatenate([s[0] for s in sums] + [s[1] for s in sums], axis=1)
        d_mixed, g_q1, g_kv1, g_a1 = back_qkv(mixed, full_b, gains[3], n1_1, d_q1, d_kv1, d_mid1)
        head1 = over_core(g_q1, g_kv1, g_out1, columns(g_a1, g_b1))

        d_delta = at_picks(d_mixed.astype(BF)).astype(F32)
        gated = gate * d_delta
        d_logit = gate * (1.0 - gate) * jnp.sum(d_delta * both0, axis=-1, keepdims=True)
        head1a = first_way(head1[..., : 2 * D], False)
        head1b = first_way(head1[..., 2 * D :], True)
        gated_low = after(gated.astype(BF), *head1a.cut, *head1b.cut)
        d_mid0, do0, g_out0, g_up0, g_down0, g_b0 = back_mlp(
            mid0, (full_a, mlp0), gains[1], (o0, n2_0, act0, slope0), gated_low, None, gated
        )
        up0, down0 = first_way(of_core(g_up0), False), first_way(of_core(g_down0), True)
        head1a = second_way(head1a.done(d_mid0), False)
        head1b = second_way(head1b.done(d_mid0), True)
        do0 = after(do0, *up0.cut, *down0.cut, *head1a.cut, *head1b.cut, *pair1.got)
        dq, d_kv = attend_back(
            own0[0], (do0, 0), (o0, 0), lse0, own0[1], own0[2], (), core_arr, lb, 0, PAIRS
        )
        d_kv0 = jnp.concatenate([d_kv[0], d_kv[1]], axis=1)
        d_rows0, g_q0, g_kv0, g_a0 = back_qkv(x_rows, full_a, gains[0], n1_0, dq, d_kv0, d_mid0)
        g_r = jnp.sum(d_logit * x_rows, axis=0)
        d_chosen = (d_rows0 + d_logit * gains[2]).astype(BF)
        grad_rows = (d_mixed + to_rows(d_chosen)).astype(BF)
        grad_sent = leave_at_once(grad_rows)
        head1a, head1b = head1a.done(grad_rows), head1b.done(grad_rows)
        up0, down0 = up0.done(grad_rows), down0.done(grad_rows)
        up0, down0 = second_way(up0, False), second_way(down0, True)
        head0a = after(of_core(g_q0, g_kv0[:, :D]), *up0.cut, *down0.cut)
        head0b = of_core(g_kv0[:, D:], g_out0, columns(g_a0, g_b0, g_r))
        head0b = after(head0b, *up0.cut, *down0.cut)
        head0a, head0b = first_way(head0a, False), first_way(head0b, True)
        up0, down0 = up0.done(*head0a.cut, *head0b.cut), down0.done(*head0a.cut, *head0b.cut)
        early = LastSum(up0, down0, head1a, head1b)
        grad_sent = [after(g, *early.cut) for g in grad_sent]
        input_grad = arrived(placed(grad_sent, chip // 2, 0)).astype(F32)
        activations = arrived(after(act_sent, *early.cut))
        head0a, head0b = head0a.done(*early.cut), head0b.done(*early.cut)
        pair1 = pair1.done(*early.cut)
        head0a, head0b = second_way(head0a, False), second_way(head0b, True)
        head0 = LastSum(head0a.done(), head0b.done())
        early = early.done(*head0.cut)
        head0 = head0.done(early)
        squares = sum(jnp.sum(v * v) for v in (early, head0, pair1))
        up0, down0, head1 = early[:, :FF], early[:, FF : 2 * FF], early[:, 2 * FF :]
        up1, down1 = pair1[:, :FF], pair1[:, FF:]

        def unmixed(up):
            return up.reshape(piece, 4, ways, piece).swapaxes(1, 2).reshape(piece, FF)

        def unpacked(down):
            return down.reshape(piece, 4, D).swapaxes(0, 1).reshape(4 * piece, D)

        shards = [
            jnp.stack([h[:, : 3 * D].reshape(piece, 3, D).transpose(1, 0, 2) for h in (head0, head1)]),
            jnp.stack([head0[:, 3 * D : 4 * D], head1[:, 3 * D : 4 * D]]),
            jnp.stack([unmixed(up0), unmixed(up1)]),
            jnp.stack([unpacked(down0), unpacked(down1)]),
            jnp.concatenate([head0[:, 4 * D : 4 * D + 3].T, head1[:, 4 * D : 4 * D + 2].T]),
        ]
        grad_norm = jnp.sqrt(all_sum(squares.reshape(1, 1))[0, 0])
        factor = 1.0 / jnp.maximum(grad_norm, 1.0)
        base_rate = math.sqrt(NPARAMS / D)
        rates = (base_rate, math.sqrt(NPARAMS * LEN / (8 * D)), base_rate, base_rate, base_rate)
        masters = (qkv_w, out_w, up_w, down_w, vectors)
        moms = (qkv_mom, out_mom, up_mom, down_mom, vec_mom)
        avgs = (qkv_avg, out_avg, up_avg, down_avg, vec_avg)
        new_w, new_m, new_z = [], [], []
        for weight, grad, mom, avg, rate in zip(masters, shards, moms, avgs, rates):
            clipped = grad * factor
            m = 0.5 * mom + clipped
            w = weight - rate * (clipped + 0.5 * m)
            new_w.append(w)
            new_m.append(m)
            new_z.append(0.5 * avg + 0.5 * w)
        return (activations, input_grad, grad_norm, *new_w, *new_m, *new_z)

    group_spec = ("y", "core")
    pos_spec = ("z", "xh", "xl")
    rows_spec = P(pos_spec, group_spec, None)
    param_specs = (
        P(None, None, every, None),
        P(None, every, None),
        P(None, every, None),
        P(None, every, None),
        P(None, every),
    )
    return jax.shard_map(
        body,
        mesh=inner,
        in_specs=(rows_spec, rows_spec, P(group_spec, None), P(group_spec)) + param_specs * 3,
        out_specs=(rows_spec, rows_spec, P()) + param_specs * 3,
        check_vma=False,
    )
```
